32 devices in a mesh: gx: 8 (over y, x, core), gy: 4 (over z).
Axes of the slice: x: 2, y: 2, z: 4, core: 2. Of those that a mesh axis runs over, the one named last changes fastest.
Arguments:
- particles: float32 [7, 524288], P(None, ('gx', 'gy')), may hold values from -3 to 3, as said below
- mig_count: int32 [32, 4], P(('gx', 'gy')), may hold values from 1 to 512, as said below
- mig_rows: int32 [32, 4, 512], P(('gx', 'gy')), may hold values from 0 to 16383, as said below
- active_ids: int32 [32, 2, 8], P(('gx', 'gy')), may hold values from 0 to 127, as said below
- active_count: int32 [32, 2], P(('gx', 'gy')), may hold values from 1 to 8, as said below
- local_nbrs: int32 [32, 2, 8, 3], P(('gx', 'gy')), may hold values from 0 to 127
- ghost_slots: int32 [32, 2, 8, 4], P(('gx', 'gy')), may hold values from 0 to 31
- export_blocks: int32 [32, 4, 8], P(('gx', 'gy')), may hold values from 0 to 127
Outputs:
- density: float32 [524288], P(('gx', 'gy'))
- accel: float32 [3, 524288], P(None, ('gx', 'gy'))
The draws below stay inside these ranges and needn't reach their ends.
Inputs may be any that keep to these rules, and one draw needn't show every extreme that they name: `mig_count`: each level's count is the same for both devices of a pair, and device 0 and its partners exchange exactly 512 at every level. `mig_rows`: the slots of one device at one level are distinct. `active_ids`: the 16 ids of one device are distinct. `active_count`: the two bins of one device hold at most 12 blocks together; device 0 holds 8 in bin 0 and 12 in all. `particles`: Rows: positions first, then mass, smoothing length, internal energy and previous density, these four positive.
All inputs are finite; a program needn't handle non-finite values.
Results may differ from the reference program's by a relative error of at most 0.00002.
Values sent between devices are 32-bit elements; how exact they have to be, the bound alone decides.
No kernel may reach another device: no remote copies, remote signals or barrier semaphores. Data moves between devices by JAX's collectives and lax.ppermute only.
A program may use at most 128 MiB of HBM per device.

```python
import math
import jax
import jax.numpy as jnp
from jax import lax

BLK = 128
NB = 128
MIG = 512
NACT = 8
TOTACT = 12
NLOC = 3
NGH = 4
SLOTS = 8
PEERS = 4
PER_DEV = 16384
PARTICLES = 524288
DEVICES = 32


def log_draw(subkey, low_end, high_end):
    unit = jax.random.uniform(subkey, (1, PARTICLES), jnp.float32)
    return low_end * jnp.exp(unit * jnp.log(high_end / low_end))


def draw_particles(key, part):
    subkeys = jax.random.split(key, 5)
    places = jnp.clip(0.5 * jax.random.normal(subkeys[0], (3, PARTICLES), jnp.float32), -3.0, 3.0)
    masses = log_draw(subkeys[1], 0.004, 0.016)
    smooth = log_draw(subkeys[2], 0.5, 1.0)
    energy = log_draw(subkeys[3], 0.5, 2.0)
    previous = log_draw(subkeys[4], 0.2, 2.0)
    return jnp.concatenate([places, masses, smooth, energy, previous], axis=0)


def draw_mig_count(key, part):
    raw_counts = jax.random.randint(key, (DEVICES, 4), 1, MIG + 1)
    raw_counts = raw_counts.at[0].set(MIG)
    device = jnp.arange(DEVICES, dtype=jnp.int32)
    partners = jnp.stack([device ^ 2 * PEERS, device ^ PEERS, device ^ 2, device ^ 1], axis=1)
    mirrored = raw_counts[partners, jnp.arange(4, dtype=jnp.int32)[None, :]]
    return jnp.maximum(raw_counts, mirrored)


def draw_mig_rows(key, part):
    subkeys = jax.random.split(key, DEVICES * 4)
    chosen = jax.vmap(lambda one_key: jax.random.permutation(one_key, PER_DEV)[:MIG])(subkeys)
    return chosen.reshape(DEVICES, 4, MIG).astype(jnp.int32)


def draw_active_ids(key, part):
    subkeys = jax.random.split(key, DEVICES)
    chosen = jax.vmap(lambda one_key: jax.random.permutation(one_key, NB)[:2 * NACT])(subkeys)
    return chosen.reshape(DEVICES, 2, NACT).astype(jnp.int32)


def draw_active_count(key, part):
    subkeys = jax.random.split(key, 2)
    first_bin = jax.random.randint(subkeys[0], (DEVICES,), 1, NACT + 1)
    second_bin = jax.random.randint(subkeys[1], (DEVICES,), 1, NACT + 1)
    second_bin = jnp.minimum(second_bin, TOTACT - first_bin)
    first_bin = first_bin.at[0].set(NACT)
    second_bin = second_bin.at[0].set(TOTACT - NACT)
    return jnp.stack([first_bin, second_bin], axis=1).astype(jnp.int32)


def touch_ends(entries, key, smallest, top_value):
    place = [jax.random.randint(jax.random.fold_in(key, axis), (), 0, length) for axis, length in enumerate(entries.shape)]
    widest = entries.shape.index(max(entries.shape))
    next_to = place[:widest] + [(place[widest] + 1) % entries.shape[widest]] + place[widest + 1:]
    return entries.at[tuple(place)].set(smallest).at[tuple(next_to)].set(top_value)


def setup_inputs(seed: int = 0) -> dict:
    arg_keys = jax.random.split(jax.random.key(seed), 9)
    return {
        "particles": draw_particles(jax.random.fold_in(arg_keys[8], 71), 0),
        "mig_count": draw_mig_count(jax.random.fold_in(arg_keys[8], 71), 0),
        "mig_rows": draw_mig_rows(jax.random.fold_in(arg_keys[8], 71), 0),
        "active_ids": draw_active_ids(jax.random.fold_in(arg_keys[8], 71), 0),
        "active_count": draw_active_count(jax.random.fold_in(arg_keys[8], 71), 0),
        "local_nbrs": touch_ends(jax.random.randint(arg_keys[5], (DEVICES, 2, NACT, NLOC), 0, NB), jax.random.fold_in(arg_keys[5], 1), 0, NB - 1).astype(jnp.int32),
        "ghost_slots": touch_ends(jax.random.randint(arg_keys[6], (DEVICES, 2, NACT, NGH), 0, PEERS * SLOTS), jax.random.fold_in(arg_keys[6], 1), 0, (PEERS * SLOTS) - 1).astype(jnp.int32),
        "export_blocks": touch_ends(jax.random.randint(arg_keys[7], (DEVICES, PEERS, SLOTS), 0, NB), jax.random.fold_in(arg_keys[7], 1), 0, NB - 1).astype(jnp.int32),
    }


KERNEL_NORM = 21.0 / (16.0 * math.pi)
GAMMA_LESS = 2.0 / 3.0

def density_tile(centre_pos, smooth, others):
    offset = centre_pos[:, :, None] - others[0:3, None, :]
    distance = jnp.sqrt(lax.optimization_barrier(jnp.sum(offset * offset, axis=0)))
    scaled = distance / smooth[:, None]
    falloff = jnp.maximum(1.0 - 0.5 * scaled, 0.0)
    square = falloff * falloff
    kernel = KERNEL_NORM / (smooth * smooth * smooth)[:, None] * (square * square) * (1.0 + 2.0 * scaled)
    return lax.optimization_barrier(jnp.sum(kernel * others[3][None, :], axis=1))

def pair_force(centre, others):
    offset = centre[0:3, :, None] - others[0:3, None, :]
    distance = jnp.sqrt(lax.optimization_barrier(jnp.sum(offset * offset, axis=0)))
    pair_smooth = 0.5 * (centre[4][:, None] + others[4][None, :])
    scaled = distance / pair_smooth
    falloff = jnp.maximum(1.0 - 0.5 * scaled, 0.0)
    inverse = 1.0 / pair_smooth
    inv_square = inverse * inverse
    gradient = -5.0 * KERNEL_NORM * (falloff * falloff * falloff) * (inv_square * inv_square * inverse)
    pressure = GAMMA_LESS * (centre[5] / centre[6])[:, None] + GAMMA_LESS * (others[5] / others[6])[None, :]
    weight = -(centre[3][:, None] * others[3][None, :]) * pressure * gradient
    pushes = weight[None] * offset
    return (lax.optimization_barrier(jnp.sum(pushes, axis=2)), -lax.optimization_barrier(jnp.sum(pushes, axis=1)))

def slot_densities(own_blocks, ghosts, slot_ids, near_ids, far_ids):

    def per_slot(inputs):
        active, near, far = inputs
        centre = own_blocks[active]
        neighbours = jnp.concatenate([centre[None, 0:4], own_blocks[near][:, 0:4], ghosts[far][:, 0:4]], axis=0)
        tile_sums = jax.vmap(lambda block_row: density_tile(centre[0:3], centre[4], block_row))(neighbours)
        return lax.optimization_barrier(jnp.sum(tile_sums, axis=0))
    return lax.map(per_slot, (slot_ids, near_ids, far_ids))

def slot_forces(own_blocks, ghosts, slot_ids, near_ids, far_ids, live_slot):

    def per_slot(inputs):
        active, near, far, alive = inputs
        centre = own_blocks[active]
        neighbours = jnp.concatenate([own_blocks[near], ghosts[far]], axis=0)
        self_push = pair_force(centre, centre)[0]
        on_centre, on_others = jax.vmap(lambda block_row: pair_force(centre, block_row))(neighbours)
        factor = jnp.where(alive, 1.0, 0.0).astype(jnp.float32)
        count_near = near.shape[0]
        centre_sum = (self_push + lax.optimization_barrier(jnp.sum(on_centre, axis=0))) * factor
        return (centre_sum, on_others[:count_near] * factor, on_others[count_near:] * factor)
    return lax.map(per_slot, (slot_ids, near_ids, far_ids, live_slot))

def migrate(current, mig_count, mig_rows):
    device = jnp.arange(DEVICES, dtype=jnp.int32)
    partners = (device ^ 2 * PEERS, device ^ PEERS, device ^ 2, device ^ 1)
    lane_ids = jnp.arange(MIG, dtype=jnp.int32)
    for section_num in range(4):
        moving_rows = mig_rows[:, section_num, :]
        outgoing = jnp.take_along_axis(current, moving_rows[None], axis=2)
        arrived = outgoing[:, partners[section_num], :]
        staying = lane_ids[None, :] < mig_count[:, section_num][:, None]
        settled = jnp.where(staying[None], arrived, outgoing)
        current = current.at[:, device[:, None], moving_rows].set(settled)
    return current

def reference(particles, mig_count, mig_rows, active_ids, active_count, local_nbrs, ghost_slots, export_blocks):
    current = migrate(particles.reshape(7, DEVICES, PER_DEV), mig_count, mig_rows)
    blocks = current.reshape(7, DEVICES, NB, BLK).transpose(1, 2, 0, 3)
    device = jnp.arange(DEVICES, dtype=jnp.int32)
    owners = (device // PEERS)[:, None] * PEERS + jnp.arange(PEERS, dtype=jnp.int32)[None, :]
    exported = export_blocks[owners[:, :, None], (device % PEERS)[:, None, None], jnp.arange(SLOTS, dtype=jnp.int32)[None, None, :]]
    slot_ids = active_ids.reshape(DEVICES, 2 * NACT)
    live_slot = (jnp.arange(NACT, dtype=jnp.int32)[None, None, :] < active_count[:, :, None]).reshape(DEVICES, 2 * NACT)
    near_ids = local_nbrs.reshape(DEVICES, 2 * NACT, NLOC)
    far_ids = ghost_slots.reshape(DEVICES, 2 * NACT, NGH)

    def fetch_ghosts(source, device_id):
        return source[owners[device_id][:, None], exported[device_id]].reshape(PEERS * SLOTS, 7, BLK)

    def densities(device_id):
        ghosts = fetch_ghosts(blocks, device_id)
        own_blocks = blocks[device_id]
        fresh = slot_densities(own_blocks, ghosts, slot_ids[device_id], near_ids[device_id], far_ids[device_id])
        previous = own_blocks[:, 6]
        chosen = slot_ids[device_id]
        return previous.at[chosen].set(jnp.where(live_slot[device_id][:, None], fresh, previous[chosen]))
    density_all = lax.map(densities, device)
    blocks = blocks.at[:, :, 6].set(density_all)

    def forces(device_id):
        ghosts = fetch_ghosts(blocks, device_id)
        own_blocks = blocks[device_id]
        on_centre, on_near, on_far = slot_forces(own_blocks, ghosts, slot_ids[device_id], near_ids[device_id], far_ids[device_id], live_slot[device_id])
        totals = jnp.zeros((NB, 3, BLK), dtype=jnp.float32).at[slot_ids[device_id]].add(on_centre)
        totals = totals.at[near_ids[device_id].reshape(-1)].add(on_near.reshape(-1, 3, BLK))
        returned = jnp.zeros((PEERS * SLOTS, 3, BLK), dtype=jnp.float32).at[far_ids[device_id].reshape(-1)].add(on_far.reshape(-1, 3, BLK))
        return (totals, returned)
    totals, returned = lax.map(forces, device)
    totals = totals.at[owners[:, :, None], exported].add(returned.reshape(DEVICES, PEERS, SLOTS, 3, BLK))
    accel = totals / blocks[:, :, 3][:, :, None, :]
    return (blocks[:, :, 6].reshape(-1), accel.transpose(2, 0, 1, 3).reshape(3, -1))
```

```python
import math

import jax
import jax.numpy as jnp
from jax import lax
from jax.experimental import pallas as pl
from jax.experimental.pallas import tpu as pltpu
from jax.sharding import PartitionSpec as P

BLK = 128
TOTACT = 12
KERNEL_NORM = 21.0 / (16.0 * math.pi)
FORCE_NORM = 5.0 * KERNEL_NORM * 32.0 * (2.0 / 3.0)
TINY = 1e-30
F32 = jnp.float32
I32 = jnp.int32
VMEM = pltpu.VMEM
SMEM = pltpu.SMEM


def call(kernel, out_shape, *args, smem=(), scratch=(), limit=16 << 20):
    in_specs = [pl.BlockSpec(memory_space=SMEM if n in smem else VMEM) for n in range(len(args))]
    return pl.pallas_call(
        kernel,
        out_shape=out_shape,
        in_specs=in_specs,
        out_specs=jax.tree.map(lambda _: pl.BlockSpec(memory_space=VMEM), out_shape),
        scratch_shapes=list(scratch),
        compiler_params=pltpu.CompilerParams(vmem_limit_bytes=limit),
    )(*args)


def shape(*dims, dtype=F32):
    return jax.ShapeDtypeStruct(dims, dtype)


def wide(row):
    return jnp.broadcast_to(row, (8, BLK))


def lanes(block):
    return pl.ds(pl.multiple_of(block * BLK, BLK), BLK)


def chunk(c):
    return slice(c * BLK, (c + 1) * BLK)


def take(values, index):
    return jnp.take_along_axis(values, index, axis=1)


def patch(values, code, tables):
    lane = code & (BLK - 1)
    which = code >> 7
    for n, table in enumerate(tables):
        values = jnp.where(which == n, take(table, lane), values)
    return values


def tables_of(ref, count, start=0):
    return [ref[:, chunk(start + c)] for c in range(count)]


def columns(state, slots):
    block = slots >> 7
    lane = slots & (BLK - 1)
    found = jnp.zeros((8, BLK), F32)
    for b in range(state.shape[1] // BLK):
        found = jnp.where(block == b, take(state[:, chunk(b)], lane), found)
    return found


def load_state(state, particles):
    state[0:7, :] = particles[...]
    state[7:8, :] = jnp.zeros((1, state.shape[1]), F32)


def first_kernel(particles, rows, out, state):
    load_state(state, particles)
    for c in range(rows.shape[1] // BLK):
        out[:, chunk(c)] = columns(state, wide(rows[0:1, chunk(c)]))


def code_table(rows, counts, level, blocks):
    mig = rows.shape[1]
    slots = rows[level : level + 1, :]
    k = lax.broadcasted_iota(I32, (1, mig), 1)
    live = k < counts[0:1, level : level + 1]
    low = jnp.where(live, k & (BLK - 1), 0).astype(F32)
    high = jnp.where(live, (k >> 7) + 1, 0).astype(F32)
    in_block = lax.broadcasted_iota(I32, (blocks, mig), 0) == (slots >> 7)
    in_lane = lax.broadcasted_iota(I32, (BLK, mig), 0) == (slots & (BLK - 1))
    left = jnp.concatenate([jnp.where(in_block, low, 0.0), jnp.where(in_block, high, 0.0)], axis=0)
    right = jnp.where(in_lane, 1.0, 0.0)
    both = lax.dot_general(
        left.astype(jnp.bfloat16),
        right.astype(jnp.bfloat16),
        (((1,), (1,)), ((), ())),
        preferred_element_type=F32,
    )
    low, high = both[:blocks], both[blocks:]
    return jnp.where(high > 0.5, (high - 1.0) * BLK + low, -1.0).astype(I32)


def code_at(table, slots):
    block = slots >> 7
    lane = slots & (BLK - 1)
    row = lax.broadcasted_iota(I32, (8, BLK), 0)
    found = jnp.full((8, BLK), -1, I32)
    for v in range(table.shape[0] // 8):
        piece = take(table[8 * v : 8 * v + 8, :], lane)
        found = jnp.where(block == row + 8 * v, piece, found)
    return jnp.max(found, axis=0, keepdims=True)


def tables_kernel(particles, rows, counts, cols, marks, early, late, state):
    mig = rows.shape[1]
    blocks = early.shape[0]
    load_state(state, particles)
    code0 = code_table(rows, counts, 0, blocks)
    code1 = code_table(rows, counts, 1, blocks)
    code2 = code_table(rows, counts, 2, blocks)
    code3 = code_table(rows, counts, 3, blocks)
    early[...] = jnp.where(code1 >= 0, code1 + mig, code0)
    late[...] = jnp.where(code3 >= 0, code3 + mig, code2)
    for c in range(mig // BLK):
        slots = [wide(rows[level : level + 1, chunk(c)]) for level in range(4)]
        marks[0:1, chunk(c)] = code_at(code0, slots[1])
        marks[1:2, chunk(c)] = code_at(early, slots[2])
        marks[2:3, chunk(c)] = code_at(early, slots[3])
        marks[3:4, chunk(c)] = code_at(code2, slots[3])
        for level in (1, 2, 3):
            cols[level - 1, :, chunk(c)] = columns(state, slots[level])


def second_kernel(cols, marks, got0, out):
    count = got0.shape[1] // BLK
    for c in range(count):
        out[:, chunk(c)] = patch(
            cols[0, :, chunk(c)], wide(marks[0:1, chunk(c)]), tables_of(got0, count)
        )


def make_export_kernel(peers, slots, meta_exports):
    def export_kernel(meta, particles, cols, marks, got0, got1, early, late, *outs):
        count = got0.shape[1] // BLK
        tables = tables_of(got0, count) + tables_of(got1, count)
        row = lax.broadcasted_iota(I32, (8, BLK), 0)
        for c in range(count):
            two = patch(cols[1, :, chunk(c)], wide(marks[1:2, chunk(c)]), tables)
            three = patch(cols[2, :, chunk(c)], wide(marks[2:3, chunk(c)]), tables)
            three = jnp.where(row == 7, wide(marks[3:4, chunk(c)]).astype(F32), three)
            for out in outs:
                out[:, chunk(c)] = two
                out[:, chunk(count + c)] = three
        me = meta[0]
        for q, out in enumerate(outs):
            for t in range(slots):
                block = meta[meta_exports + (me ^ q) * slots + t]
                out[:, chunk(2 * count + t)] = early_block(
                    particles, early, late, tables, block
                )

    return export_kernel


def early_block(particles, early, late, tables, block):
    values = jnp.concatenate(
        [particles[:, lanes(block)], late[pl.ds(block, 1), :].astype(F32)], axis=0
    )
    row = lax.broadcasted_iota(I32, (8, BLK), 0)
    patched = patch(values, wide(early[pl.ds(block, 1), :]), tables)
    return jnp.where(row == 7, values, patched)


def make_density_kernel(peers, slots, lay):
    def density_kernel(
        meta, particles, early, late, got0, got1, *refs
    ):
        sent = refs[:peers]
        near, density = refs[peers : peers + 2]
        exports = refs[peers + 2 : 2 * peers + 2]
        late_three, ghosts = refs[2 * peers + 2 :]
        count = got0.shape[1] // BLK
        blocks = density.shape[0]
        row = lax.broadcasted_iota(I32, (8, BLK), 0)
        me = meta[0]
        first = tables_of(got0, count) + tables_of(got1, count)

        for q in range(peers):
            tables = tables_of(sent[q ^ 2], count)
            for c in range(count):
                values = sent[q][:, chunk(count + c)]
                code = wide(values[7:8, :]).astype(I32)
                late_three[q, :, chunk(c)] = patch(values, code, tables)

        def settle(values, q):
            code = wide(values[7:8, :]).astype(I32)
            tables = tables_of(sent[q ^ 2], count)
            tables += [late_three[q ^ 1, :, chunk(c)] for c in range(count)]
            return patch(values, code, tables)

        for q in range(peers):
            for t in range(slots):
                ghosts[:, chunk(q * slots + t)] = settle(sent[q][:, chunk(2 * count + t)], q)

        last = [got0[6:7, chunk(c)] for c in range(count)]
        last += [got1[6:7, chunk(c)] for c in range(count)]
        later = [sent[2][6:7, chunk(c)] for c in range(count)]
        later += [late_three[1, 6:7, chunk(c)] for c in range(count)]
        for b in range(blocks):
            density[b : b + 1, :] = particles[6:7, chunk(b)]
        last = [wide(x) for x in last]
        later = [wide(x) for x in later]
        for v in range(blocks // 8):
            part = slice(8 * v, 8 * v + 8)
            values = patch(density[part, :], early[part, :], last)
            density[part, :] = patch(values, late[part, :], later)

        live = meta[1] + meta[2]

        def slot_of(n):
            return jnp.where(n < meta[1], n, n - meta[1] + lay["nact"])

        def gather_slot(n, _):
            s = slot_of(n)
            a = meta[lay["ids"] + s]
            near[n, :, 0, :] = settle(early_block(particles, early, late, first, a), 0)
            for t in range(lay["nloc"]):
                b = meta[lay["nbrs"] + s * lay["nloc"] + t]
                near[n, :, 1 + t, :] = settle(early_block(particles, early, late, first, b), 0)
            for t in range(lay["ngh"]):
                g = meta[lay["far"] + s * lay["ngh"] + t] ^ (me * slots)
                near[n, :, 1 + lay["nloc"] + t, :] = ghosts[:, lanes(g)]
            return 0

        lax.fori_loop(0, live, gather_slot, 0)

        def slot_density(n, _):
            a = meta[lay["ids"] + slot_of(n)]
            x, y, z, m = (near[n, q] for q in range(4))
            cx, cy, cz, h = (wide(near[n, q, 0:1, :]) for q in (0, 1, 2, 4))
            half = 0.5 / h
            sums = [jnp.zeros((8, BLK), F32) for _ in range(4)]
            for r in range(BLK):
                dx = cx - pltpu.roll(x, r, 1)
                dy = cy - pltpu.roll(y, r, 1)
                dz = cz - pltpu.roll(z, r, 1)
                square = dx * dx + dy * dy + dz * dz
                t = square * lax.rsqrt(jnp.maximum(square, TINY)) * half
                fall = jnp.maximum(1.0 - t, 0.0)
                fall = fall * fall
                sums[r % 4] += fall * fall * (1.0 + 4.0 * t) * pltpu.roll(m, r, 1)
            total = (sums[0] + sums[1]) + (sums[2] + sums[3])
            total = jnp.sum(total, axis=0, keepdims=True)
            h = h[0:1, :]
            density[pl.ds(a, 1), :] = total * (KERNEL_NORM / (h * h * h))
            return 0

        lax.fori_loop(0, live, slot_density, 0)

        for q in range(peers):
            for t in range(slots):
                b = meta[lay["exports"] + (me ^ q) * slots + t]
                exports[q][t : t + 1, :] = density[pl.ds(b, 1), :]

    return density_kernel


def make_force_kernel(peers, slots, lay):
    def force_kernel(meta, near, density, *refs):
        rho = refs[:peers]
        totals = refs[peers]
        returns = refs[peers + 1 : 2 * peers + 1]
        far_rho, work, back = refs[2 * peers + 1 :]
        me = meta[0]
        for q in range(peers):
            far_rho[q * slots : (q + 1) * slots, :] = rho[q][...]
        totals[...] = jnp.zeros_like(totals)
        back[...] = jnp.zeros_like(back)
        live = meta[1] + meta[2]

        def slot_force(n, _):
            s = jnp.where(n < meta[1], n, n - meta[1] + lay["nact"])
            a = meta[lay["ids"] + s]
            nbrs = [meta[lay["nbrs"] + s * lay["nloc"] + t] for t in range(lay["nloc"])]
            far = [
                meta[lay["far"] + s * lay["ngh"] + t] ^ (me * slots) for t in range(lay["ngh"])
            ]
            for t, b in enumerate([a] + nbrs):
                work[0, t : t + 1, :] = density[pl.ds(b, 1), :]
            for t, g in enumerate(far):
                work[0, 1 + len(nbrs) + t : 2 + len(nbrs) + t, :] = far_rho[pl.ds(g, 1), :]
            x, y, z, m, h, u = (near[n, q] for q in range(6))
            p = u / work[0]
            cx, cy, cz, cm, ch, cp = (wide(v[0:1, :]) for v in (x, y, z, m, h, p))
            centre = [jnp.zeros((8, BLK), F32) for _ in range(3)]
            others = [jnp.zeros((8, BLK), F32) for _ in range(3)]
            for r in range(BLK):
                d = [c - pltpu.roll(v, r, 1) for c, v in ((cx, x), (cy, y), (cz, z))]
                square = d[0] * d[0] + d[1] * d[1] + d[2] * d[2]
                inverse = 1.0 / (ch + pltpu.roll(h, r, 1))
                t = square * lax.rsqrt(jnp.maximum(square, TINY)) * inverse
                fall = jnp.maximum(1.0 - t, 0.0)
                inv2 = inverse * inverse
                weight = fall * fall * fall * (inv2 * inv2 * inverse)
                weight = weight * (cp + pltpu.roll(p, r, 1)) * (cm * pltpu.roll(m, r, 1))
                for k in range(3):
                    push = weight * d[k]
                    centre[k] = centre[k] + push
                    others[k] = others[k] + pltpu.roll(push, (BLK - r) % BLK, 1)
            scale_centre = FORCE_NORM / cm[0:1, :]
            scale_others = -FORCE_NORM / m
            for k in range(3):
                work[k] = others[k] * scale_others
            for k in range(3):
                work[k, 0:1, :] = jnp.sum(centre[k], axis=0, keepdims=True) * scale_centre
            for t, b in enumerate([a] + nbrs):
                totals[0:3, lanes(b)] += work[0:3, t, :]
            for t, g in enumerate(far):
                back[0:3, lanes(g)] += work[0:3, 1 + len(nbrs) + t, :]
            return 0

        lax.fori_loop(0, live, slot_force, 0)
        for q in range(peers):
            returns[q][...] = back[:, q * slots * BLK : (q + 1) * slots * BLK]

    return force_kernel


def make_final_kernel(peers, slots, lay):
    def final_kernel(meta, totals, *refs):
        got = refs[:peers]
        out, work = refs[peers:]
        me = meta[0]
        work[...] = totals[...]
        for q in range(peers):
            for t in range(slots):
                b = meta[lay["exports"] + (me ^ q) * slots + t]
                work[:, lanes(b)] += got[q][:, chunk(t)]
        out[...] = work[0:3, :]

    return final_kernel


def crossed(block, axis, bits):
    size = lax.axis_size(axis)
    return lax.ppermute(block, axis, [(i, i ^ bits) for i in range(size) if i ^ bits < size])


def shards(
    particles, mig_count, mig_rows, active_ids, active_count, local_nbrs, ghost_slots, export_blocks
):
    peers = lax.axis_size("gy")
    slots = export_blocks.shape[2]
    per_dev = particles.shape[1]
    blocks = per_dev // BLK
    mig = mig_rows.shape[2]
    rows = mig_rows[0]
    nact = active_ids.shape[2]
    total = active_ids.shape[1] * nact
    lay = {"nact": nact, "nloc": local_nbrs.shape[3], "ngh": ghost_slots.shape[3], "ids": 3}
    lay["nbrs"] = lay["ids"] + total
    lay["far"] = lay["nbrs"] + total * lay["nloc"]
    lay["exports"] = lay["far"] + total * lay["ngh"]
    meta = jnp.concatenate(
        [
            lax.axis_index("gy").astype(I32).reshape(1),
            active_count.reshape(-1),
            active_ids.reshape(-1),
            local_nbrs.reshape(-1),
            ghost_slots.reshape(-1),
            export_blocks.reshape(-1),
        ]
    )
    state = VMEM((8, per_dev), F32)
    sent0 = call(first_kernel, shape(8, mig), particles, rows, scratch=[state])
    got0 = crossed(sent0, "gx", 2)
    cols, marks, early, late = call(
        tables_kernel,
        [
            shape(3, 8, mig),
            shape(8, mig, dtype=I32),
            shape(blocks, BLK, dtype=I32),
            shape(blocks, BLK, dtype=I32),
        ],
        particles,
        rows,
        mig_count,
        scratch=[state],
    )
    sent1 = call(second_kernel, shape(8, mig), cols, marks, got0)
    got1 = crossed(sent1, "gx", 1)
    packs = call(
        make_export_kernel(peers, slots, lay["exports"]),
        [shape(8, 2 * mig + slots * BLK)] * peers,
        meta,
        particles,
        cols,
        marks,
        got0,
        got1,
        early,
        late,
        smem=(0,),
    )
    order = list(range(peers - 1, 0, -1))
    arrived = {q: crossed(packs[q], "gy", q) for q in order}
    sent = [packs[0]] + [arrived[q] for q in range(1, peers)]
    wide_total = peers * slots * BLK
    results = call(
        make_density_kernel(peers, slots, lay),
        [shape(TOTACT, 8, 8, BLK), shape(blocks, BLK)] + [shape(slots, BLK)] * peers,
        meta,
        particles,
        early,
        late,
        got0,
        got1,
        *sent,
        smem=(0,),
        scratch=[VMEM((peers, 8, mig), F32), VMEM((8, wide_total), F32)],
    )
    near, density, exports = results[0], results[1], results[2:]
    arrived = {q: crossed(exports[q], "gy", q) for q in order}
    rho = [exports[0]] + [arrived[q] for q in range(1, peers)]
    results = call(
        make_force_kernel(peers, slots, lay),
        [shape(8, per_dev)] + [shape(8, slots * BLK)] * peers,
        meta,
        near,
        density,
        *rho,
        smem=(0,),
        scratch=[VMEM((peers * slots, BLK), F32), VMEM((8, 8, BLK), F32), VMEM((8, wide_total), F32)],
    )
    totals, returns = results[0], results[1:]
    arrived = {q: crossed(returns[q], "gy", q) for q in order}
    got = [returns[0]] + [arrived[q] for q in range(1, peers)]
    accel = call(
        make_final_kernel(peers, slots, lay),
        shape(3, per_dev),
        meta,
        totals,
        *got,
        smem=(0,),
        scratch=[state],
    )
    return density.reshape(-1), accel


def solution(mesh):
    both = ("gx", "gy")
    placed = (
        P(None, both),
        P(both, None),
        P(both, None, None),
        P(both, None, None),
        P(both, None),
        P(both, None, None, None),
        P(both, None, None, None),
        P(both, None, None),
    )
    return jax.shard_map(
        shards,
        mesh=mesh,
        in_specs=placed,
        out_specs=(P(both), P(None, both)),
        check_vma=False,
    )
```

```python
import math

import jax
import jax.numpy as jnp
from jax import lax
from jax.experimental import pallas as pl
from jax.experimental.pallas import tpu as pltpu
from jax.sharding import PartitionSpec as P

BLK = 128
TOTACT = 12
KERNEL_NORM = 21.0 / (16.0 * math.pi)
FORCE_NORM = 5.0 * KERNEL_NORM * 32.0 * (2.0 / 3.0)
TINY = 1e-30
F32 = jnp.float32
I32 = jnp.int32
VMEM = pltpu.VMEM
SMEM = pltpu.SMEM
HBM = pltpu.HBM
DMA = pltpu.SemaphoreType.DMA


def call(kernel, out_shape, *args, smem=(), hbm=(), scratch=(), limit=16 << 20):
    def space(n):
        return SMEM if n in smem else HBM if n in hbm else VMEM

    return pl.pallas_call(
        kernel,
        out_shape=out_shape,
        in_specs=[pl.BlockSpec(memory_space=space(n)) for n in range(len(args))],
        out_specs=jax.tree.map(lambda _: pl.BlockSpec(memory_space=VMEM), out_shape),
        scratch_shapes=list(scratch),
        compiler_params=pltpu.CompilerParams(vmem_limit_bytes=limit),
    )(*args)


def shape(*dims, dtype=F32):
    return jax.ShapeDtypeStruct(dims, dtype)


def wide(row):
    return jnp.broadcast_to(row, (8, BLK))


def lanes(block):
    return pl.ds(pl.multiple_of(block * BLK, BLK), BLK)


def chunk(c):
    return slice(c * BLK, (c + 1) * BLK)


def take(values, index):
    return jnp.take_along_axis(values, index, axis=1)


def patch(values, code, tables):
    lane = code & (BLK - 1)
    which = code >> 7
    for n, table in enumerate(tables):
        values = jnp.where(which == n, take(table, lane), values)
    return values


def tables_of(ref, count, start=0):
    return [ref[:, chunk(start + c)] for c in range(count)]


def columns(state, slots):
    block = slots >> 7
    lane = slots & (BLK - 1)
    found = jnp.zeros((8, BLK), F32)
    for b in range(state.shape[1] // BLK):
        found = jnp.where(block == b, take(state[:, chunk(b)], lane), found)
    return found


def fetch(sources, targets, sems):
    copies = [
        pltpu.make_async_copy(a, b, sems.at[n]) for n, (a, b) in enumerate(zip(sources, targets))
    ]
    for copy in copies:
        copy.start()
    return copies


def fetch_scratch(arrays):
    return [SMEM(a.shape, I32) for a in arrays] + [DMA((len(arrays),))]


PIECES = 4


def first_kernel(particles, mig_rows, out, state, rows, sems):
    per_dev = particles.shape[1]
    size = per_dev // PIECES
    mig = mig_rows.shape[2]
    index_copy = pltpu.make_async_copy(mig_rows.at[0], rows, sems.at[PIECES])
    index_copy.start()
    copies = []
    for p in range(PIECES):
        part = slice(p * size, (p + 1) * size)
        copy = pltpu.make_async_copy(
            particles.at[:, part], state.at[pl.ds(0, 7), part], sems.at[p]
        )
        copy.start()
        copies.append(copy)
    index_copy.wait()
    slots = [wide(rows[0:1, chunk(c)]) for c in range(mig // BLK)]
    found = [jnp.zeros((8, BLK), F32) for _ in slots]
    for p, copy in enumerate(copies):
        copy.wait()
        for b in range(p * size // BLK, (p + 1) * size // BLK):
            values = state[:, chunk(b)]
            for c, s in enumerate(slots):
                picked = take(values, s & (BLK - 1))
                found[c] = jnp.where((s >> 7) == b, picked, found[c])
    for c, values in enumerate(found):
        out[:, chunk(c)] = values


def code_table(rows, counts, level, blocks):
    mig = rows.shape[1]
    slots = rows[level : level + 1, :]
    k = lax.broadcasted_iota(I32, (1, mig), 1)
    live = k < counts[0:1, level : level + 1]
    low = jnp.where(live, k & (BLK - 1), 0).astype(F32)
    high = jnp.where(live, (k >> 7) + 1, 0).astype(F32)
    in_block = lax.broadcasted_iota(I32, (blocks, mig), 0) == (slots >> 7)
    in_lane = lax.broadcasted_iota(I32, (BLK, mig), 0) == (slots & (BLK - 1))
    left = jnp.concatenate([jnp.where(in_block, low, 0.0), jnp.where(in_block, high, 0.0)], axis=0)
    right = jnp.where(in_lane, 1.0, 0.0)
    both = lax.dot_general(
        left.astype(jnp.bfloat16),
        right.astype(jnp.bfloat16),
        (((1,), (1,)), ((), ())),
        preferred_element_type=F32,
    )
    low, high = both[:blocks], both[blocks:]
    return jnp.where(high > 0.5, (high - 1.0) * BLK + low, -1.0).astype(I32)


def code_at(table, slots):
    block = slots >> 7
    lane = slots & (BLK - 1)
    row = lax.broadcasted_iota(I32, (8, BLK), 0)
    found = jnp.full((8, BLK), -1, I32)
    for v in range(table.shape[0] // 8):
        piece = take(table[8 * v : 8 * v + 8, :], lane)
        found = jnp.where(block == row + 8 * v, piece, found)
    return jnp.max(found, axis=0, keepdims=True)


def early_tables_kernel(state, rows, counts, cols, marks, codes):
    mig = rows.shape[1]
    blocks = codes.shape[1]
    for level in range(2):
        codes[level] = code_table(rows, counts, level, blocks)
    for c in range(mig // BLK):
        slots = wide(rows[1:2, chunk(c)])
        marks[0:1, chunk(c)] = code_at(codes.at[0], slots)
        cols[:, chunk(c)] = columns(state, slots)


def late_tables_kernel(state, rows, counts, codes, after, cols, marks, early, late):
    mig = rows.shape[1]
    blocks = codes.shape[1]
    code2 = code_table(rows, counts, 2, blocks)
    code3 = code_table(rows, counts, 3, blocks)
    early[...] = jnp.where(codes[1] >= 0, codes[1] + mig, codes[0])
    late[...] = jnp.where(code3 >= 0, code3 + mig, code2)
    for c in range(mig // BLK):
        two, three = (wide(rows[level : level + 1, chunk(c)]) for level in (2, 3))
        marks[1:2, chunk(c)] = code_at(early, two)
        marks[2:3, chunk(c)] = code_at(early, three)
        marks[3:4, chunk(c)] = code_at(code2, three)
        cols[0, :, chunk(c)] = columns(state, two)
        cols[1, :, chunk(c)] = columns(state, three)


def second_kernel(cols, marks, got0, out):
    count = got0.shape[1] // BLK
    tables = tables_of(got0, count)
    for c in range(count):
        out[:, chunk(c)] = patch(cols[:, chunk(c)], wide(marks[0:1, chunk(c)]), tables)


def early_block(state, early, late, tables, block):
    row = lax.broadcasted_iota(I32, (8, BLK), 0)
    patched = patch(state[:, lanes(block)], wide(early[pl.ds(block, 1), :]), tables)
    return jnp.where(row == 7, wide(late[pl.ds(block, 1), :]).astype(F32), patched)


def export_kernel(state, cols, marks, got0, got1, early, late, exports, *refs):
    outs, (exported, sems) = refs[:-2], refs[-2:]
    copies = fetch([exports], [exported], sems)
    count = got0.shape[1] // BLK
    tables = tables_of(got0, count) + tables_of(got1, count)
    row = lax.broadcasted_iota(I32, (8, BLK), 0)
    for c in range(count):
        two = patch(cols[0, :, chunk(c)], wide(marks[1:2, chunk(c)]), tables)
        three = patch(cols[1, :, chunk(c)], wide(marks[2:3, chunk(c)]), tables)
        three = jnp.where(row == 7, wide(marks[3:4, chunk(c)]).astype(F32), three)
        for out in outs:
            out[:, chunk(c)] = two
            out[:, chunk(count + c)] = three
    me = lax.axis_index("gy")
    for copy in copies:
        copy.wait()
    for q, out in enumerate(outs):
        for t in range(exported.shape[2]):
            block = exported[0, me ^ q, t]
            out[:, chunk(2 * count + t)] = early_block(state, early, late, tables, block)


def live_slot(counts, n, nact):
    second = n >= counts[0, 0]
    return jnp.where(second, 1, 0), jnp.where(second, jnp.minimum(n - counts[0, 0], nact - 1), n)


def own_kernel(state, got0, got1, early, late, ids, counts, nbrs, own, density):
    count = got0.shape[1] // BLK
    blocks = density.shape[0]
    tables = tables_of(got0, count) + tables_of(got1, count)
    last = [wide(table[6:7, :]) for table in tables]
    for b in range(blocks):
        density[b : b + 1, :] = state[6:7, chunk(b)]
    for v in range(blocks // 8):
        part = slice(8 * v, 8 * v + 8)
        density[part, :] = patch(density[part, :], early[part, :], last)
    nact = ids.shape[2]

    def pick(n, _):
        which, i = live_slot(counts, n, nact)
        wanted = [ids[0, which, i]] + [nbrs[0, which, i, t] for t in range(nbrs.shape[3])]
        for t, block in enumerate(wanted):
            own[n, t] = early_block(state, early, late, tables, block)
        return 0

    lax.fori_loop(0, counts[0, 0] + counts[0, 1], pick, 0)


def spread(rows, out):
    columns_of = jnp.transpose(jnp.concatenate((rows + rows)[:8], axis=0))
    for k in range(len(rows)):
        out[k] = jnp.broadcast_to(columns_of[:, k : k + 1], (BLK, BLK))


def in_turn(live, prepare, work, first, second):
    prepare(0, first)

    def step(p, _):
        n = 2 * p
        prepare(n + 1, second)
        work(n, first)
        prepare(jnp.minimum(n + 2, TOTACT - 1), first)
        work(n + 1, second)
        return 0

    lax.fori_loop(0, (live + 1) // 2, step, 0)


def density_sums(near, n, centre, sums):
    for g in range(BLK // 8):
        part = slice(8 * g, 8 * g + 8)
        cx, cy, cz, half = (centre[k, part, :] for k in range(4))
        total = None
        for t in range(8):
            x, y, z, m = (wide(near[n, k, t : t + 1, :]) for k in range(4))
            dx, dy, dz = cx - x, cy - y, cz - z
            square = dx * dx + dy * dy + dz * dz
            ratio = square * lax.rsqrt(jnp.maximum(square, TINY)) * half
            fall = jnp.maximum(1.0 - ratio, 0.0)
            fall = fall * fall
            term = fall * fall * (1.0 + 4.0 * ratio) * m
            total = term if total is None else total + term
        sums[n, part, :] = total


def make_density_kernel(peers, slots):
    def density_kernel(own, before, late, ids, counts, far, exports, *refs):
        sent = refs[:peers]
        near, density = refs[peers : peers + 2]
        outs = refs[peers + 2 : 2 * peers + 2]
        (late_three, ghosts, first, second, sums, fresh, *small) = refs[2 * peers + 2 :]
        copies = fetch([ids, counts, far, exports], small[:4], small[4])
        ids, counts, far, exports = small[:4]
        count = late_three.shape[2] // BLK
        blocks = density.shape[0]
        me = lax.axis_index("gy")

        for q in range(peers):
            tables = tables_of(sent[q ^ 2], count)
            for c in range(count):
                values = sent[q][:, chunk(count + c)]
                code = wide(values[7:8, :]).astype(I32)
                late_three[q, :, chunk(c)] = patch(values, code, tables)

        def settle(values, q):
            code = wide(values[7:8, :]).astype(I32)
            tables = tables_of(sent[q ^ 2], count)
            tables += [late_three[q ^ 1, :, chunk(c)] for c in range(count)]
            return patch(values, code, tables)

        for q in range(peers):
            for t in range(slots):
                ghosts[:, chunk(q * slots + t)] = settle(sent[q][:, chunk(2 * count + t)], q)

        later = [sent[2][6:7, chunk(c)] for c in range(count)]
        later = [wide(x) for x in later + [late_three[1, 6:7, chunk(c)] for c in range(count)]]
        for v in range(blocks // 8):
            part = slice(8 * v, 8 * v + 8)
            density[part, :] = patch(before[part, :], late[part, :], later)

        for copy in copies:
            copy.wait()
        live = counts[0, 0] + counts[0, 1]
        nact = ids.shape[2]
        inner = own.shape[1]

        def gather(n, _):
            which, i = live_slot(counts, n, nact)
            for t in range(inner):
                near[n, :, t, :] = settle(own[n, t], 0)
            for t in range(far.shape[3]):
                g = far[0, which, i, t] ^ (me * slots)
                near[n, :, inner + t, :] = ghosts[:, lanes(g)]
            return 0

        lax.fori_loop(0, live, gather, 0)

        def prepare(n, buffer):
            rows = [near[n, k, 0:1, :] for k in range(3)]
            spread(rows + [0.5 / near[n, 4, 0:1, :]], buffer)

        in_turn(live, prepare, lambda n, b: density_sums(near, n, b, sums), first, second)
        for n in range(TOTACT):
            h = near[n, 4, 0:1, :]
            total = jnp.sum(jnp.transpose(sums[n]), axis=0, keepdims=True)
            fresh[n : n + 1, :] = total * (KERNEL_NORM / (h * h * h))

        def place(n, _):
            which, i = live_slot(counts, n, nact)
            density[pl.ds(ids[0, which, i], 1), :] = fresh[pl.ds(n, 1), :]
            return 0

        lax.fori_loop(0, live, place, 0)
        for q in range(peers):
            for t in range(slots):
                outs[q][t : t + 1, :] = density[pl.ds(exports[0, me ^ q, t], 1), :]

    return density_kernel


def force_sums(near, press, n, centre, sums, others, tiles):
    pushed = {t: [None] * 3 for t in tiles}
    for g in range(BLK // 8):
        part = slice(8 * g, 8 * g + 8)
        cx, cy, cz, cm, ch, cp = (centre[k, part, :] for k in range(6))
        total = [None] * 3
        for t in tiles:
            x, y, z, m, h = (wide(near[n, k, t : t + 1, :]) for k in range(5))
            apart = [cx - x, cy - y, cz - z]
            square = apart[0] * apart[0] + apart[1] * apart[1] + apart[2] * apart[2]
            inverse = 1.0 / (ch + h)
            distance = square * lax.rsqrt(jnp.maximum(square, TINY))
            fall = jnp.maximum(1.0 - distance * inverse, 0.0)
            inv2 = inverse * inverse
            weight = fall * fall * fall * (inv2 * inv2 * inverse)
            weight = weight * (cp + wide(press[n, t : t + 1, :])) * (cm * m)
            for k in range(3):
                push = weight * apart[k]
                total[k] = push if total[k] is None else total[k] + push
                if t > 0:
                    pushed[t][k] = push if pushed[t][k] is None else pushed[t][k] + push
        for k in range(3):
            sums[n, k, part, :] = total[k]
    for t in tiles:
        if t > 0:
            for k in range(3):
                others[n, k, 8 * t : 8 * t + 8, :] = pushed[t][k]


def forces(near, press, live, first, second, sums, others, rows, tiles):
    def prepare(n, buffer):
        spread([near[n, k, 0:1, :] for k in range(5)] + [press[n, 0:1, :]], buffer)

    def work(n, buffer):
        force_sums(near, press, n, buffer, sums, others, tiles)

    in_turn(live, prepare, work, first, second)
    for n in range(TOTACT):
        for k in range(3):
            scale = FORCE_NORM / near[n, 3, 0:1, :]
            total = jnp.sum(jnp.transpose(sums[n, k]), axis=0, keepdims=True)
            rows[n, k, 0:1, :] = total * scale
            for t in tiles:
                if t > 0:
                    total = jnp.sum(others[n, k, 8 * t : 8 * t + 8, :], axis=0, keepdims=True)
                    scale = -FORCE_NORM / near[n, 3, t : t + 1, :]
                    rows[n, k, t : t + 1, :] = total * scale


def force_scratch():
    return [
        VMEM((6, BLK, BLK), F32),
        VMEM((6, BLK, BLK), F32),
        VMEM((TOTACT, 3, BLK, BLK), F32),
        VMEM((TOTACT, 3, 8 * 8, BLK), F32),
        VMEM((TOTACT, 8, 8, BLK), F32),
        VMEM((TOTACT, 8, BLK), F32),
        VMEM((TOTACT, 8, BLK), F32),
    ]


def inner_kernel(near, density, ids, counts, nbrs, totals, *refs):
    first, second, sums, others, rows, press, rho = refs
    totals[...] = jnp.zeros_like(totals)
    live = counts[0, 0] + counts[0, 1]
    nact = ids.shape[2]
    inner = 1 + nbrs.shape[3]

    def blocks_of(n):
        which, i = live_slot(counts, n, nact)
        return [ids[0, which, i]] + [nbrs[0, which, i, t] for t in range(nbrs.shape[3])]

    def look_up(n, _):
        for t, block in enumerate(blocks_of(n)):
            rho[n, t : t + 1, :] = density[pl.ds(block, 1), :]
        return 0

    lax.fori_loop(0, live, look_up, 0)
    for n in range(TOTACT):
        press[n] = near[n, 5] / rho[n]
    forces(near, press, live, first, second, sums, others, rows, tuple(range(inner)))

    def place(n, _):
        for t, block in enumerate(blocks_of(n)):
            totals[0:3, lanes(block)] += rows[n, 0:3, t, :]
        return 0

    lax.fori_loop(0, live, place, 0)


def make_outer_kernel(peers, slots):
    def outer_kernel(near, density, ids, counts, far, *refs):
        got = refs[:peers]
        centre = refs[peers]
        returns = refs[peers + 1 : 2 * peers + 1]
        (first, second, sums, others, rows, press, rho, far_rho, back, *small) = refs[
            2 * peers + 1 :
        ]
        copies = fetch([ids, counts, far], small[:3], small[3])
        ids, counts, far = small[:3]
        for q in range(peers):
            far_rho[q * slots : (q + 1) * slots, :] = got[q][...]
        back[...] = jnp.zeros_like(back)
        me = lax.axis_index("gy")
        nact = ids.shape[2]
        ngh = far.shape[3]
        tiles = tuple(range(8 - ngh, 8))
        for copy in copies:
            copy.wait()
        live = counts[0, 0] + counts[0, 1]

        def look_up(n, _):
            which, i = live_slot(counts, n, nact)
            rho[n, 0:1, :] = density[pl.ds(ids[0, which, i], 1), :]
            for t in range(ngh):
                g = far[0, which, i, t] ^ (me * slots)
                rho[n, 8 - ngh + t : 9 - ngh + t, :] = far_rho[pl.ds(g, 1), :]
            return 0

        lax.fori_loop(0, live, look_up, 0)
        for n in range(TOTACT):
            press[n] = near[n, 5] / rho[n]
        forces(near, press, live, first, second, sums, others, rows, tiles)

        def place(n, _):
            which, i = live_slot(counts, n, nact)
            centre[n, 0:3, :] = rows[n, 0:3, 0, :]
            for t in range(ngh):
                g = far[0, which, i, t] ^ (me * slots)
                back[0:3, lanes(g)] += rows[n, 0:3, 8 - ngh + t, :]
            return 0

        lax.fori_loop(0, live, place, 0)
        for q in range(peers):
            returns[q][...] = back[:, q * slots * BLK : (q + 1) * slots * BLK]

    return outer_kernel


def make_final_kernel(peers, slots):
    def final_kernel(totals, centre, ids, counts, exports, *refs):
        got = refs[:peers]
        out, work, *small = refs[peers:]
        copies = fetch([ids, counts, exports], small[:3], small[3])
        ids, counts, exports = small[:3]
        work[...] = totals[...]
        me = lax.axis_index("gy")
        nact = ids.shape[2]
        for copy in copies:
            copy.wait()

        def place(n, _):
            which, i = live_slot(counts, n, nact)
            work[0:3, lanes(ids[0, which, i])] += centre[n, 0:3, :]
            return 0

        lax.fori_loop(0, counts[0, 0] + counts[0, 1], place, 0)
        for q in range(peers):
            for t in range(slots):
                work[0:3, lanes(exports[0, me ^ q, t])] += got[q][0:3, chunk(t)]
        out[...] = work[0:3, :]

    return final_kernel


def crossed(block, axis, bits):
    size = lax.axis_size(axis)
    return lax.ppermute(block, axis, [(i, i ^ bits) for i in range(size) if i ^ bits < size])


def exchanged(parts):
    arrived = {q: crossed(parts[q], "gy", q) for q in range(len(parts) - 1, 0, -1)}
    return [parts[0]] + [arrived[q] for q in range(1, len(parts))]


def shards(
    particles, mig_count, mig_rows, active_ids, active_count, local_nbrs, ghost_slots, export_blocks
):
    peers = lax.axis_size("gy")
    slots = export_blocks.shape[2]
    per_dev = particles.shape[1]
    blocks = per_dev // BLK
    mig = mig_rows.shape[2]
    inner = 1 + local_nbrs.shape[3]
    wide_total = peers * slots * BLK

    sent0, state, rows = call(
        first_kernel,
        [shape(8, mig), shape(8, per_dev), shape(4, mig, dtype=I32)],
        particles,
        mig_rows,
        hbm=(0, 1),
        scratch=[DMA((PIECES + 1,))],
    )
    got0 = crossed(sent0, "gx", 2)
    cols1, marks1, codes = call(
        early_tables_kernel,
        [shape(8, mig), shape(8, mig, dtype=I32), shape(2, blocks, BLK, dtype=I32)],
        state,
        rows,
        mig_count,
    )
    sent1 = call(second_kernel, shape(8, mig), cols1, marks1, got0)
    got1 = crossed(sent1, "gx", 1)
    table = shape(blocks, BLK, dtype=I32)
    cols, marks, early, late = call(
        late_tables_kernel,
        [shape(2, 8, mig), shape(8, mig, dtype=I32), table, table],
        state,
        rows,
        mig_count,
        codes,
        sent1,
    )
    packs = call(
        export_kernel,
        [shape(8, 2 * mig + slots * BLK)] * peers,
        state,
        cols,
        marks,
        got0,
        got1,
        early,
        late,
        export_blocks,
        scratch=fetch_scratch([export_blocks]),
    )
    sent = exchanged(packs)
    own, before = call(
        own_kernel,
        [shape(TOTACT, inner, 8, BLK), shape(blocks, BLK)],
        state,
        got0,
        got1,
        early,
        late,
        active_ids,
        active_count,
        local_nbrs,
        smem=(5, 6, 7),
    )
    indices = [active_ids, active_count, ghost_slots, export_blocks]
    near, density, *exports = call(
        make_density_kernel(peers, slots),
        [shape(TOTACT, 8, 8, BLK), shape(blocks, BLK)] + [shape(slots, BLK)] * peers,
        own,
        before,
        late,
        *indices,
        *sent,
        scratch=[
            VMEM((peers, 8, mig), F32),
            VMEM((8, wide_total), F32),
            VMEM((4, BLK, BLK), F32),
            VMEM((4, BLK, BLK), F32),
            VMEM((TOTACT, BLK, BLK), F32),
            VMEM((TOTACT, BLK), F32),
        ]
        + fetch_scratch(indices),
    )
    rho = exchanged(exports)
    totals = call(
        inner_kernel,
        shape(8, per_dev),
        near,
        density,
        active_ids,
        active_count,
        local_nbrs,
        smem=(2, 3, 4),
        scratch=force_scratch(),
    )
    indices = [active_ids, active_count, ghost_slots]
    centre, *returns = call(
        make_outer_kernel(peers, slots),
        [shape(TOTACT, 8, BLK)] + [shape(8, slots * BLK)] * peers,
        near,
        density,
        *indices,
        *rho,
        scratch=force_scratch()
        + [VMEM((peers * slots, BLK), F32), VMEM((8, wide_total), F32)]
        + fetch_scratch(indices),
    )
    got = exchanged(returns)
    indices = [active_ids, active_count, export_blocks]
    accel = call(
        make_final_kernel(peers, slots),
        shape(3, per_dev),
        totals,
        centre,
        *indices,
        *got,
        scratch=[VMEM((8, per_dev), F32)] + fetch_scratch(indices),
    )
    return density.reshape(-1), accel


def solution(mesh):
    both = ("gx", "gy")
    placed = (
        P(None, both),
        P(both, None),
        P(both, None, None),
        P(both, None, None),
        P(both, None),
        P(both, None, None, None),
        P(both, None, None, None),
        P(both, None, None),
    )
    return jax.shard_map(
        shards,
        mesh=mesh,
        in_specs=placed,
        out_specs=(P(both), P(None, both)),
        check_vma=False,
    )
```

```python
import math

import jax
import jax.numpy as jnp
from jax import lax
from jax.experimental import pallas as pl
from jax.experimental.pallas import tpu as pltpu
from jax.sharding import PartitionSpec as P

BLK = 128
TOTACT = 12
KERNEL_NORM = 21.0 / (16.0 * math.pi)
FORCE_NORM = 5.0 * KERNEL_NORM * 32.0 * (2.0 / 3.0)
TINY = 1e-30
F32 = jnp.float32
I32 = jnp.int32
VMEM = pltpu.VMEM
SMEM = pltpu.SMEM
DMA = pltpu.SemaphoreType.DMA


def call(kernel, out_shape, *args, smem=(), scratch=(), limit=16 << 20, cost=0):
    def space(n):
        return SMEM if n in smem else VMEM

    return pl.pallas_call(
        kernel,
        out_shape=out_shape,
        in_specs=[pl.BlockSpec(memory_space=space(n)) for n in range(len(args))],
        out_specs=jax.tree.map(lambda _: pl.BlockSpec(memory_space=VMEM), out_shape),
        scratch_shapes=list(scratch),
        compiler_params=pltpu.CompilerParams(vmem_limit_bytes=limit),
        cost_estimate=pl.CostEstimate(flops=0, transcendentals=0, bytes_accessed=cost)
        if cost
        else None,
    )(*args)


def shape(*dims, dtype=F32):
    return jax.ShapeDtypeStruct(dims, dtype)


def wide(row):
    return jnp.broadcast_to(row, (8, BLK))


def lanes(block):
    return pl.ds(pl.multiple_of(block * BLK, BLK), BLK)


def chunk(c):
    return slice(c * BLK, (c + 1) * BLK)


def take(values, index):
    return jnp.take_along_axis(values, index, axis=1)


def patch(values, code, tables):
    lane = code & (BLK - 1)
    which = code >> 7
    for n, table in enumerate(tables):
        values = jnp.where(which == n, take(table, lane), values)
    return values


def tables_of(ref, count, start=0):
    return [ref[:, chunk(start + c)] for c in range(count)]


def columns(state, slots):
    block = slots >> 7
    lane = slots & (BLK - 1)
    found = jnp.zeros((8, BLK), F32)
    for b in range(state.shape[1] // BLK):
        found = jnp.where(block == b, take(state[:, chunk(b)], lane), found)
    return found


def fetch(sources, targets, sems):
    copies = [
        pltpu.make_async_copy(a, b, sems.at[n]) for n, (a, b) in enumerate(zip(sources, targets))
    ]
    for copy in copies:
        copy.start()
    return copies


def fetch_scratch(arrays):
    return [SMEM(a.shape, I32) for a in arrays] + [DMA((len(arrays),))]


def first_kernel(state, mig_rows, out, rows):
    rows[...] = mig_rows[...]
    for c in range(mig_rows.shape[2] // BLK):
        out[:, chunk(c)] = columns(state, wide(mig_rows[0, 0:1, chunk(c)]))


def code_table(mig_rows, level, blocks):
    mig = mig_rows.shape[2]
    slots = mig_rows[0, level : level + 1, :]
    k = lax.broadcasted_iota(I32, (1, mig), 1)
    low = (k & (BLK - 1)).astype(F32)
    high = ((k >> 7) + 1).astype(F32)
    in_block = lax.broadcasted_iota(I32, (blocks, mig), 0) == (slots >> 7)
    in_lane = lax.broadcasted_iota(I32, (BLK, mig), 0) == (slots & (BLK - 1))
    left = jnp.concatenate([jnp.where(in_block, low, 0.0), jnp.where(in_block, high, 0.0)], axis=0)
    right = jnp.where(in_lane, 1.0, 0.0)
    both = lax.dot_general(
        left.astype(jnp.bfloat16),
        right.astype(jnp.bfloat16),
        (((1,), (1,)), ((), ())),
        preferred_element_type=F32,
    )
    low, high = both[:blocks], both[blocks:]
    return jnp.where(high > 0.5, (high - 1.0) * BLK + low, -1.0).astype(I32)


def codes_kernel(mig_rows, codes):
    for level in range(4):
        codes[level] = code_table(mig_rows, level, codes.shape[1])


def code_at(table, slots):
    block = slots >> 7
    lane = slots & (BLK - 1)
    row = lax.broadcasted_iota(I32, (8, BLK), 0)
    found = jnp.full((8, BLK), -1, I32)
    for v in range(table.shape[0] // 8):
        piece = take(table[8 * v : 8 * v + 8, :], lane)
        found = jnp.where(block == row + 8 * v, piece, found)
    return jnp.max(found, axis=0, keepdims=True)


def early_tables_kernel(state, mig_rows, codes, counts, exports, cols, marks, tables, exports_out):
    mig = mig_rows.shape[2]
    exports_out[...] = exports[...]
    valid = []
    for level in range(4):
        code = codes[level]
        valid.append(jnp.where(code < counts[0:1, level : level + 1], code, -1))
    tables[0] = jnp.where(valid[1] >= 0, valid[1] + mig, valid[0])
    tables[1] = jnp.where(valid[3] >= 0, valid[3] + mig, valid[2])
    tables[2] = valid[2]
    tables[3] = valid[0]
    for c in range(mig // BLK):
        slots = wide(mig_rows[0, 1:2, chunk(c)])
        marks[0:1, chunk(c)] = code_at(tables.at[3], slots)
        cols[:, chunk(c)] = columns(state, slots)


def late_tables_kernel(
    state, mig_rows, tables, exports, after, cols, marks, raw, code_rows, exported, sems
):
    copies = fetch([exports], [exported], sems)
    for c in range(mig_rows.shape[2] // BLK):
        two, three = (wide(mig_rows[0, level : level + 1, chunk(c)]) for level in (2, 3))
        marks[1:2, chunk(c)] = code_at(tables.at[0], two)
        marks[2:3, chunk(c)] = code_at(tables.at[0], three)
        marks[3:4, chunk(c)] = code_at(tables.at[2], three)
        cols[0, :, chunk(c)] = columns(state, two)
        cols[1, :, chunk(c)] = columns(state, three)
    for copy in copies:
        copy.wait()
    me = lax.axis_index("gy")
    peers, slots = exports.shape[1:]
    row = lax.broadcasted_iota(I32, (8, BLK), 0)
    for q in range(peers):
        for t in range(slots):
            block = exported[0, me ^ q, t]
            code = wide(tables[1, pl.ds(block, 1), :]).astype(F32)
            raw[:, chunk(q * slots + t)] = jnp.where(row == 7, code, state[:, lanes(block)])
            code_rows[q, t : t + 1, :] = tables[0, pl.ds(block, 1), :]


def second_kernel(cols, marks, got0, out):
    count = got0.shape[1] // BLK
    tables = tables_of(got0, count)
    for c in range(count):
        out[:, chunk(c)] = patch(cols[:, chunk(c)], wide(marks[0:1, chunk(c)]), tables)


def early_block(state, codes, tables, block):
    row = lax.broadcasted_iota(I32, (8, BLK), 0)
    patched = patch(state[:, lanes(block)], wide(codes[0, pl.ds(block, 1), :]), tables)
    return jnp.where(row == 7, wide(codes[1, pl.ds(block, 1), :]).astype(F32), patched)


def export_kernel(cols, marks, got0, got1, raw, code_rows, *outs):
    count = got0.shape[1] // BLK
    slots = code_rows.shape[1]
    tables = tables_of(got0, count) + tables_of(got1, count)
    row = lax.broadcasted_iota(I32, (8, BLK), 0)
    for c in range(count):
        two = patch(cols[0, :, chunk(c)], wide(marks[1:2, chunk(c)]), tables)
        three = patch(cols[1, :, chunk(c)], wide(marks[2:3, chunk(c)]), tables)
        three = jnp.where(row == 7, wide(marks[3:4, chunk(c)]).astype(F32), three)
        for out in outs:
            out[:, chunk(c)] = two
            out[:, chunk(count + c)] = three
    for q, out in enumerate(outs):
        for t in range(slots):
            values = raw[:, chunk(q * slots + t)]
            patched = patch(values, wide(code_rows[q, t : t + 1, :]), tables)
            out[:, chunk(2 * count + t)] = jnp.where(row == 7, values, patched)


def live_slot(counts, n, nact):
    second = n >= counts[0, 0]
    return jnp.where(second, 1, 0), jnp.where(second, jnp.minimum(n - counts[0, 0], nact - 1), n)


def own_kernel(state, got0, got1, codes, ids, counts, nbrs, own, density):
    count = got0.shape[1] // BLK
    blocks = density.shape[0]
    tables = tables_of(got0, count) + tables_of(got1, count)
    last = [wide(table[6:7, :]) for table in tables]
    for b in range(blocks):
        density[b : b + 1, :] = state[6:7, chunk(b)]
    for v in range(blocks // 8):
        part = slice(8 * v, 8 * v + 8)
        density[part, :] = patch(density[part, :], codes[0, part, :], last)
    nact = ids.shape[2]

    for n in range(TOTACT):
        which, i = live_slot(counts, n, nact)
        wanted = [ids[0, which, i]] + [nbrs[0, which, i, t] for t in range(nbrs.shape[3])]
        for t, block in enumerate(wanted):
            own[n, t] = early_block(state, codes, tables, block)


def spread(rows, out):
    columns_of = jnp.transpose(jnp.concatenate((rows + rows)[:8], axis=0))
    for k in range(len(rows)):
        out[k] = jnp.broadcast_to(columns_of[:, k : k + 1], (BLK, BLK))


def in_turn(live, prepare, work, first, second, start=0, stop=TOTACT):
    prepare(start, first)

    def step(p, _):
        n = 2 * p
        prepare(n + 1, second)
        work(n, first)
        prepare(jnp.minimum(n + 2, TOTACT - 1), first)
        work(n + 1, second)
        return 0

    lax.fori_loop(start // 2, (jnp.minimum(live, stop) + 1) // 2, step, 0)


def density_sums(near, n, centre, sums):
    for g in range(BLK // 8):
        part = slice(8 * g, 8 * g + 8)
        cx, cy, cz, half = (centre[k, part, :] for k in range(4))
        total = None
        for t in range(8):
            x, y, z, m = (wide(near[n, k, t : t + 1, :]) for k in range(4))
            dx, dy, dz = cx - x, cy - y, cz - z
            square = dx * dx + dy * dy + dz * dz
            ratio = square * lax.rsqrt(jnp.maximum(square, TINY)) * half
            fall = jnp.maximum(1.0 - ratio, 0.0)
            fall = fall * fall
            term = fall * fall * (1.0 + 4.0 * ratio) * m
            total = term if total is None else total + term
        sums[n, part, :] = total


def make_density_kernel(peers, slots):
    def density_kernel(own, before, codes, ids, counts, far, exports, *refs):
        sent = by_partner(refs[:peers])
        near, density = refs[peers : peers + 2]
        outs = refs[peers + 2 : 2 * peers + 2]
        (late_three, ghosts, first, second, sums, fresh, *small) = refs[2 * peers + 2 :]
        copies = fetch([ids, counts, far, exports], small[:4], small[4])
        ids, counts, far, exports = small[:4]
        count = late_three.shape[2] // BLK
        blocks = density.shape[0]
        me = lax.axis_index("gy")

        for q in range(peers):
            tables = tables_of(sent[q ^ 2], count)
            for c in range(count):
                values = sent[q][:, chunk(count + c)]
                code = wide(values[7:8, :]).astype(I32)
                late_three[q, :, chunk(c)] = patch(values, code, tables)

        def settle(values, q):
            code = wide(values[7:8, :]).astype(I32)
            tables = tables_of(sent[q ^ 2], count)
            tables += [late_three[q ^ 1, :, chunk(c)] for c in range(count)]
            return patch(values, code, tables)

        for q in range(peers):
            for t in range(slots):
                ghosts[:, chunk(q * slots + t)] = settle(sent[q][:, chunk(2 * count + t)], q)

        later = [sent[2][6:7, chunk(c)] for c in range(count)]
        later = [wide(x) for x in later + [late_three[1, 6:7, chunk(c)] for c in range(count)]]
        for v in range(blocks // 8):
            part = slice(8 * v, 8 * v + 8)
            density[part, :] = patch(before[part, :], codes[1, part, :], later)

        for copy in copies:
            copy.wait()
        live = counts[0, 0] + counts[0, 1]
        nact = ids.shape[2]
        inner = own.shape[1]

        for n in range(TOTACT):
            which, i = live_slot(counts, n, nact)
            for t in range(inner):
                near[n, :, t, :] = settle(own[n, t], 0)
            for t in range(far.shape[3]):
                g = far[0, which, i, t] ^ (me * slots)
                near[n, :, inner + t, :] = ghosts[:, lanes(g)]

        def prepare(n, buffer):
            rows = [near[n, k, 0:1, :] for k in range(3)]
            spread(rows + [0.5 / near[n, 4, 0:1, :]], buffer)

        in_turn(live, prepare, lambda n, b: density_sums(near, n, b, sums), first, second)
        for n in range(TOTACT):
            h = near[n, 4, 0:1, :]
            total = jnp.sum(jnp.transpose(sums[n]), axis=0, keepdims=True)
            fresh[n : n + 1, :] = total * (KERNEL_NORM / (h * h * h))

        def place(n, _):
            which, i = live_slot(counts, n, nact)
            density[pl.ds(ids[0, which, i], 1), :] = fresh[pl.ds(n, 1), :]
            return 0

        lax.fori_loop(0, live, place, 0)
        for q in range(peers):
            for t in range(slots):
                outs[q][t : t + 1, :] = density[pl.ds(exports[0, me ^ q, t], 1), :]

    return density_kernel


def force_sums(near, press, n, centre, sums, others, tiles):
    pushed = {t: [None] * 3 for t in tiles}
    for g in range(BLK // 8):
        part = slice(8 * g, 8 * g + 8)
        cx, cy, cz, cm, ch, cp = (centre[k, part, :] for k in range(6))
        total = [None] * 3
        for t in tiles:
            x, y, z, m, h = (wide(near[n, k, t : t + 1, :]) for k in range(5))
            apart = [cx - x, cy - y, cz - z]
            square = apart[0] * apart[0] + apart[1] * apart[1] + apart[2] * apart[2]
            inverse = 1.0 / (ch + h)
            distance = square * lax.rsqrt(jnp.maximum(square, TINY))
            fall = jnp.maximum(1.0 - distance * inverse, 0.0)
            inv2 = inverse * inverse
            weight = fall * fall * fall * (inv2 * inv2 * inverse)
            weight = weight * (cp + wide(press[n, t : t + 1, :])) * (cm * m)
            for k in range(3):
                push = weight * apart[k]
                total[k] = push if total[k] is None else total[k] + push
                if t > 0:
                    pushed[t][k] = push if pushed[t][k] is None else pushed[t][k] + push
        for k in range(3):
            sums[n, k, part, :] = total[k]
    for t in tiles:
        if t > 0:
            for k in range(3):
                others[n, k, 8 * t : 8 * t + 8, :] = pushed[t][k]


def forces(near, press, live, first, second, sums, others, rows, tiles, start=0, stop=TOTACT):
    def prepare(n, buffer):
        spread([near[n, k, 0:1, :] for k in range(5)] + [press[n, 0:1, :]], buffer)

    def work(n, buffer):
        force_sums(near, press, n, buffer, sums, others, tiles)

    in_turn(live, prepare, work, first, second, start, stop)
    for n in range(start, stop):
        for k in range(3):
            scale = FORCE_NORM / near[n, 3, 0:1, :]
            total = jnp.sum(jnp.transpose(sums[n, k]), axis=0, keepdims=True)
            rows[n, k, 0:1, :] = total * scale
            for t in tiles:
                if t > 0:
                    total = jnp.sum(others[n, k, 8 * t : 8 * t + 8, :], axis=0, keepdims=True)
                    scale = -FORCE_NORM / near[n, 3, t : t + 1, :]
                    rows[n, k, t : t + 1, :] = total * scale


def force_scratch():
    return [
        VMEM((6, BLK, BLK), F32),
        VMEM((6, BLK, BLK), F32),
        VMEM((TOTACT, 3, BLK, BLK), F32),
        VMEM((TOTACT, 3, 8 * 8, BLK), F32),
        VMEM((TOTACT, 8, 8, BLK), F32),
        VMEM((TOTACT, 8, BLK), F32),
        VMEM((TOTACT, 8, BLK), F32),
    ]


def inner_forces(near, density, ids, counts, nbrs, totals, refs, start, stop):
    first, second, sums, others, rows, press, rho = refs
    live = counts[0, 0] + counts[0, 1]
    nact = ids.shape[2]
    inner = 1 + nbrs.shape[3]

    def blocks_of(n):
        which, i = live_slot(counts, n, nact)
        return [ids[0, which, i]] + [nbrs[0, which, i, t] for t in range(nbrs.shape[3])]

    for n in range(start, stop):
        for t, block in enumerate(blocks_of(n)):
            rho[n, t : t + 1, :] = density[pl.ds(block, 1), :]
    for n in range(start, stop):
        press[n] = near[n, 5] / rho[n]
    tiles = tuple(range(inner))
    forces(near, press, live, first, second, sums, others, rows, tiles, start, stop)

    def place(n, _):
        for t, block in enumerate(blocks_of(n)):
            totals[0:3, lanes(block)] += rows[n, 0:3, t, :]
        return 0

    lax.fori_loop(start, jnp.minimum(live, stop), place, 0)


HALF = TOTACT // 2


def inner_kernel(near, density, ids, counts, nbrs, totals, density_out, *refs):
    density_out[...] = density[...]
    totals[...] = jnp.zeros_like(totals)
    inner_forces(near, density, ids, counts, nbrs, totals, refs, 0, HALF)


def inner_rest_kernel(near, density, ids, counts, nbrs, before, centre, totals, *refs):
    totals[...] = before[...]
    inner_forces(near, density, ids, counts, nbrs, totals, refs, HALF, TOTACT)

    def place(n, _):
        which, i = live_slot(counts, n, ids.shape[2])
        totals[0:3, lanes(ids[0, which, i])] += centre[n, 0:3, :]
        return 0

    lax.fori_loop(0, counts[0, 0] + counts[0, 1], place, 0)


def make_outer_kernel(peers, slots):
    def outer_kernel(near, density, after, ids, counts, far, *refs):
        got = by_partner(refs[:peers])
        centre = refs[peers]
        returns = refs[peers + 1 : 2 * peers + 1]
        (first, second, sums, others, rows, press, rho, far_rho, back, *small) = refs[
            2 * peers + 1 :
        ]
        copies = fetch([ids, counts, far], small[:3], small[3])
        ids, counts, far = small[:3]
        for q in range(peers):
            far_rho[q * slots : (q + 1) * slots, :] = got[q][...]
        back[...] = jnp.zeros_like(back)
        me = lax.axis_index("gy")
        nact = ids.shape[2]
        ngh = far.shape[3]
        tiles = tuple(range(8 - ngh, 8))
        for copy in copies:
            copy.wait()
        live = counts[0, 0] + counts[0, 1]

        for n in range(TOTACT):
            which, i = live_slot(counts, n, nact)
            rho[n, 0:1, :] = density[pl.ds(ids[0, which, i], 1), :]
            for t in range(ngh):
                g = far[0, which, i, t] ^ (me * slots)
                rho[n, 8 - ngh + t : 9 - ngh + t, :] = far_rho[pl.ds(g, 1), :]
        for n in range(TOTACT):
            press[n] = near[n, 5] / rho[n]
        forces(near, press, live, first, second, sums, others, rows, tiles)

        def place(n, _):
            which, i = live_slot(counts, n, nact)
            centre[n, 0:3, :] = rows[n, 0:3, 0, :]
            for t in range(ngh):
                g = far[0, which, i, t] ^ (me * slots)
                back[0:3, lanes(g)] += rows[n, 0:3, 8 - ngh + t, :]
            return 0

        lax.fori_loop(0, live, place, 0)
        for q in range(peers):
            returns[q][...] = back[:, q * slots * BLK : (q + 1) * slots * BLK]

    return outer_kernel


def make_final_kernel(peers, slots):
    def final_kernel(totals, exports, *refs):
        got = by_partner(refs[:peers])
        out, *small = refs[peers:]
        copies = fetch([exports], small[:1], small[1])
        exports = small[0]
        out[...] = totals[0:3, :]
        me = lax.axis_index("gy")
        for copy in copies:
            copy.wait()
        for q in range(peers):
            for t in range(slots):
                out[0:3, lanes(exports[0, me ^ q, t])] += got[q][0:3, chunk(t)]

    return final_kernel


def crossed(block, axis, bits):
    size = lax.axis_size(axis)
    return lax.ppermute(block, axis, [(i, i ^ bits) for i in range(size) if i ^ bits < size])


def exchanged(parts):
    return [parts[0]] + [crossed(parts[q], "gy", q) for q in range(len(parts) - 1, 0, -1)]


def by_partner(refs):
    return [refs[0]] + list(refs[:0:-1])


def shards(
    particles, mig_count, mig_rows, active_ids, active_count, local_nbrs, ghost_slots, export_blocks
):
    peers = lax.axis_size("gy")
    slots = export_blocks.shape[2]
    per_dev = particles.shape[1]
    blocks = per_dev // BLK
    mig = mig_rows.shape[2]
    inner = 1 + local_nbrs.shape[3]
    wide_total = peers * slots * BLK

    state = jnp.pad(particles, ((0, 1), (0, 0)))
    sent0, rows = call(
        first_kernel, [shape(8, mig), shape(*mig_rows.shape, dtype=I32)], state, mig_rows
    )
    codes = call(codes_kernel, shape(4, blocks, BLK, dtype=I32), rows)
    got0 = crossed(sent0, "gx", 2)
    cols1, marks1, tables, export_ids = call(
        early_tables_kernel,
        [
            shape(8, mig),
            shape(8, mig, dtype=I32),
            shape(4, blocks, BLK, dtype=I32),
            shape(*export_blocks.shape, dtype=I32),
        ],
        state,
        rows,
        codes,
        mig_count,
        export_blocks,
    )
    sent1 = call(second_kernel, shape(8, mig), cols1, marks1, got0)
    got1 = crossed(sent1, "gx", 1)
    cols, marks, raw, code_rows = call(
        late_tables_kernel,
        [
            shape(2, 8, mig),
            shape(8, mig, dtype=I32),
            shape(8, wide_total),
            shape(peers, slots, BLK, dtype=I32),
        ],
        state,
        rows,
        tables,
        export_ids,
        sent1,
        scratch=fetch_scratch([export_ids]),
    )
    packs = call(
        export_kernel,
        [shape(8, 2 * mig + slots * BLK)] * peers,
        cols,
        marks,
        got0,
        got1,
        raw,
        code_rows,
    )
    sent = exchanged(packs)
    own, before = call(
        own_kernel,
        [shape(TOTACT, inner, 8, BLK), shape(blocks, BLK)],
        state,
        got0,
        got1,
        tables,
        active_ids,
        active_count,
        local_nbrs,
        smem=(4, 5, 6),
    )
    indices = [active_ids, active_count, ghost_slots, export_ids]
    near, density, *exports = call(
        make_density_kernel(peers, slots),
        [shape(TOTACT, 8, 8, BLK), shape(blocks, BLK)] + [shape(slots, BLK)] * peers,
        own,
        before,
        tables,
        *indices,
        *sent,
        scratch=[
            VMEM((peers, 8, mig), F32),
            VMEM((8, wide_total), F32),
            VMEM((4, BLK, BLK), F32),
            VMEM((4, BLK, BLK), F32),
            VMEM((TOTACT, BLK, BLK), F32),
            VMEM((TOTACT, BLK), F32),
        ]
        + fetch_scratch(indices),
    )
    rho = exchanged(exports)
    totals, density_out = call(
        inner_kernel,
        [shape(8, per_dev), shape(blocks, BLK)],
        near,
        density,
        active_ids,
        active_count,
        local_nbrs,
        smem=(2, 3, 4),
        scratch=force_scratch(),
    )
    indices = [active_ids, active_count, ghost_slots]
    centre, *returns = call(
        make_outer_kernel(peers, slots),
        [shape(TOTACT, 8, BLK)] + [shape(8, slots * BLK)] * peers,
        near,
        density,
        totals,
        *indices,
        *rho,
        scratch=force_scratch()
        + [VMEM((peers * slots, BLK), F32), VMEM((8, wide_total), F32)]
        + fetch_scratch(indices),
    )
    got = exchanged(returns)
    totals = call(
        inner_rest_kernel,
        shape(8, per_dev),
        near,
        density,
        active_ids,
        active_count,
        local_nbrs,
        totals,
        centre,
        smem=(2, 3, 4),
        scratch=force_scratch(),
    )
    accel = call(
        make_final_kernel(peers, slots),
        shape(3, per_dev),
        totals,
        export_ids,
        *got,
        scratch=fetch_scratch([export_ids]),
    )
    return density_out.reshape(-1), accel


def solution(mesh):
    both = ("gx", "gy")
    placed = (
        P(None, both),
        P(both, None),
        P(both, None, None),
        P(both, None, None),
        P(both, None),
        P(both, None, None, None),
        P(both, None, None, None),
        P(both, None, None),
    )
    return jax.shard_map(
        shards,
        mesh=mesh,
        in_specs=placed,
        out_specs=(P(both), P(None, both)),
        check_vma=False,
    )
```

```python
import math

import jax
import jax.numpy as jnp
from jax import lax
from jax.experimental import pallas as pl
from jax.experimental.pallas import tpu as pltpu
from jax.sharding import PartitionSpec as P

BLK = 128
TOTACT = 12
KERNEL_NORM = 21.0 / (16.0 * math.pi)
FORCE_NORM = 5.0 * KERNEL_NORM * 32.0 * (2.0 / 3.0)
TINY = 1e-30
F32 = jnp.float32
I32 = jnp.int32
VMEM = pltpu.VMEM
SMEM = pltpu.SMEM
DMA = pltpu.SemaphoreType.DMA


def call(kernel, out_shape, *args, smem=(), scratch=(), limit=16 << 20, cost=0):
    def space(n):
        return SMEM if n in smem else VMEM

    return pl.pallas_call(
        kernel,
        out_shape=out_shape,
        in_specs=[pl.BlockSpec(memory_space=space(n)) for n in range(len(args))],
        out_specs=jax.tree.map(lambda _: pl.BlockSpec(memory_space=VMEM), out_shape),
        scratch_shapes=list(scratch),
        compiler_params=pltpu.CompilerParams(vmem_limit_bytes=limit),
        cost_estimate=pl.CostEstimate(flops=0, transcendentals=0, bytes_accessed=cost)
        if cost
        else None,
    )(*args)


def shape(*dims, dtype=F32):
    return jax.ShapeDtypeStruct(dims, dtype)


def wide(row):
    return jnp.broadcast_to(row, (8, BLK))


def lanes(block):
    return pl.ds(pl.multiple_of(block * BLK, BLK), BLK)


def chunk(c):
    return slice(c * BLK, (c + 1) * BLK)


def take(values, index):
    return jnp.take_along_axis(values, index, axis=1)


def patch(values, code, tables):
    lane = code & (BLK - 1)
    which = code >> 7
    for n, table in enumerate(tables):
        values = jnp.where(which == n, take(table, lane), values)
    return values


def tables_of(ref, count, start=0):
    return [ref[:, chunk(start + c)] for c in range(count)]


def columns(state, slots):
    block = slots >> 7
    lane = slots & (BLK - 1)
    found = jnp.zeros((8, BLK), F32)
    for b in range(state.shape[1] // BLK):
        found = jnp.where(block == b, take(state[:, chunk(b)], lane), found)
    return found


def fetch(sources, targets, sems):
    copies = [
        pltpu.make_async_copy(a, b, sems.at[n]) for n, (a, b) in enumerate(zip(sources, targets))
    ]
    for copy in copies:
        copy.start()
    return copies


def fetch_scratch(arrays):
    return [SMEM(a.shape, I32) for a in arrays] + [DMA((len(arrays),))]


def first_kernel(particles, ints, out, state):
    state[0:7, :] = particles[...]
    state[7:8, :] = jnp.zeros((1, state.shape[1]), F32)
    for c in range(ints.shape[1] // BLK):
        out[:, chunk(c)] = columns(state, wide(ints[0:1, chunk(c)]))


def code_table(ints, level, blocks):
    mig = ints.shape[1]
    slots = ints[level : level + 1, :]
    k = lax.broadcasted_iota(I32, (1, mig), 1)
    low = (k & (BLK - 1)).astype(F32)
    high = ((k >> 7) + 1).astype(F32)
    in_block = lax.broadcasted_iota(I32, (blocks, mig), 0) == (slots >> 7)
    in_lane = lax.broadcasted_iota(I32, (BLK, mig), 0) == (slots & (BLK - 1))
    left = jnp.concatenate([jnp.where(in_block, low, 0.0), jnp.where(in_block, high, 0.0)], axis=0)
    right = jnp.where(in_lane, 1.0, 0.0)
    both = lax.dot_general(
        left.astype(jnp.bfloat16),
        right.astype(jnp.bfloat16),
        (((1,), (1,)), ((), ())),
        preferred_element_type=F32,
    )
    low, high = both[:blocks], both[blocks:]
    return jnp.where(high > 0.5, (high - 1.0) * BLK + low, -1.0).astype(I32)


def codes_kernel(ints, codes):
    for level in range(4):
        codes[level] = code_table(ints, level, codes.shape[1])


def code_at(table, slots):
    block = slots >> 7
    lane = slots & (BLK - 1)
    row = lax.broadcasted_iota(I32, (8, BLK), 0)
    found = jnp.full((8, BLK), -1, I32)
    for v in range(table.shape[0] // 8):
        piece = take(table[8 * v : 8 * v + 8, :], lane)
        found = jnp.where(block == row + 8 * v, piece, found)
    return jnp.max(found, axis=0, keepdims=True)


def early_tables_kernel(state, ints, codes, cols, marks, tables):
    mig = ints.shape[1]
    valid = []
    for level in range(4):
        code = codes[level]
        valid.append(jnp.where(code < ints[4:5, level : level + 1], code, -1))
    tables[0] = jnp.where(valid[1] >= 0, valid[1] + mig, valid[0])
    tables[1] = jnp.where(valid[3] >= 0, valid[3] + mig, valid[2])
    tables[2] = valid[2]
    tables[3] = valid[0]
    for c in range(mig // BLK):
        slots = wide(ints[1:2, chunk(c)])
        marks[0:1, chunk(c)] = code_at(tables.at[3], slots)
        cols[:, chunk(c)] = columns(state, slots)


def late_tables_kernel(
    state, ints, tables, after, cols, marks, raw, code_rows, exported, sems
):
    peers, slots, _ = code_rows.shape
    copies = fetch([ints.at[pl.ds(8, peers), pl.ds(0, BLK)]], [exported], sems)
    for c in range(ints.shape[1] // BLK):
        two, three = (wide(ints[level : level + 1, chunk(c)]) for level in (2, 3))
        marks[1:2, chunk(c)] = code_at(tables.at[0], two)
        marks[2:3, chunk(c)] = code_at(tables.at[0], three)
        marks[3:4, chunk(c)] = code_at(tables.at[2], three)
        cols[0, :, chunk(c)] = columns(state, two)
        cols[1, :, chunk(c)] = columns(state, three)
    for copy in copies:
        copy.wait()
    me = lax.axis_index("gy")
    row = lax.broadcasted_iota(I32, (8, BLK), 0)
    for q in range(peers):
        for t in range(slots):
            block = exported[me ^ q, t]
            code = wide(tables[1, pl.ds(block, 1), :]).astype(F32)
            raw[:, chunk(q * slots + t)] = jnp.where(row == 7, code, state[:, lanes(block)])
            code_rows[q, t : t + 1, :] = tables[0, pl.ds(block, 1), :]


def second_kernel(cols, marks, got0, out):
    count = got0.shape[1] // BLK
    tables = tables_of(got0, count)
    for c in range(count):
        out[:, chunk(c)] = patch(cols[:, chunk(c)], wide(marks[0:1, chunk(c)]), tables)


def early_block(state, codes, tables, block):
    row = lax.broadcasted_iota(I32, (8, BLK), 0)
    patched = patch(state[:, lanes(block)], wide(codes[0, pl.ds(block, 1), :]), tables)
    return jnp.where(row == 7, wide(codes[1, pl.ds(block, 1), :]).astype(F32), patched)


def export_kernel(cols, marks, got0, got1, raw, code_rows, *outs):
    count = got0.shape[1] // BLK
    slots = code_rows.shape[1]
    tables = tables_of(got0, count) + tables_of(got1, count)
    row = lax.broadcasted_iota(I32, (8, BLK), 0)
    for c in range(count):
        two = patch(cols[0, :, chunk(c)], wide(marks[1:2, chunk(c)]), tables)
        three = patch(cols[1, :, chunk(c)], wide(marks[2:3, chunk(c)]), tables)
        three = jnp.where(row == 7, wide(marks[3:4, chunk(c)]).astype(F32), three)
        for out in outs:
            out[:, chunk(c)] = two
            out[:, chunk(count + c)] = three
    for q, out in enumerate(outs):
        for t in range(slots):
            values = raw[:, chunk(q * slots + t)]
            patched = patch(values, wide(code_rows[q, t : t + 1, :]), tables)
            out[:, chunk(2 * count + t)] = jnp.where(row == 7, values, patched)


def live_slot(counts, n, nact):
    second = n >= counts[0, 0]
    return jnp.where(second, 1, 0), jnp.where(second, jnp.minimum(n - counts[0, 0], nact - 1), n)


def own_kernel(state, got0, got1, codes, ids, counts, nbrs, own, density):
    count = got0.shape[1] // BLK
    blocks = density.shape[0]
    tables = tables_of(got0, count) + tables_of(got1, count)
    last = [wide(table[6:7, :]) for table in tables]
    for b in range(blocks):
        density[b : b + 1, :] = state[6:7, chunk(b)]
    for v in range(blocks // 8):
        part = slice(8 * v, 8 * v + 8)
        density[part, :] = patch(density[part, :], codes[0, part, :], last)
    nact = ids.shape[2]

    for n in range(TOTACT):
        which, i = live_slot(counts, n, nact)
        wanted = [ids[0, which, i]] + [nbrs[0, which, i, t] for t in range(nbrs.shape[3])]
        for t, block in enumerate(wanted):
            own[n, t] = early_block(state, codes, tables, block)


def spread(rows, *outs):
    columns_of = jnp.transpose(jnp.concatenate((rows + rows)[:8], axis=0))
    for k in range(len(rows)):
        values = jnp.broadcast_to(columns_of[:, k : k + 1], (BLK, BLK))
        for out in outs:
            out[k] = values


def pair_sums(near, n, centre, sums, inside, outside):
    local = inside.shape[1] // BLK
    for g in range(BLK // 8):
        part = slice(8 * g, 8 * g + 8)
        cx, cy, cz, cm, ch = (centre[k, part, :] for k in range(5))
        half = 0.5 / ch
        total = None
        for t in range(8):
            x, y, z, m, h = (wide(near[n, k, t : t + 1, :]) for k in range(5))
            dx, dy, dz = cx - x, cy - y, cz - z
            square = dx * dx + dy * dy + dz * dz
            distance = square * lax.rsqrt(jnp.maximum(square, TINY))
            fall = jnp.maximum(1.0 - distance * half, 0.0)
            fall2 = fall * fall
            term = fall2 * fall2 * (1.25 - fall) * m
            total = term if total is None else total + term
            inverse = 1.0 / (ch + h)
            inv2 = inverse * inverse
            slope = jnp.maximum(inverse - distance * inv2, 0.0)
            weight = slope * slope * slope * inv2 * (cm * m)
            if t < local:
                row = 8 * (g * local + t)
                inside[n, row : row + 8, :] = weight
            else:
                row = 8 * (g * (8 - local) + t - local)
                outside[n, row : row + 8, :] = weight
        sums[n, part, :] = total


def back_sums(near, n, centre, press, outside, others):
    far = outside.shape[1] // BLK
    first = 8 - far
    ghost = [[wide(near[n, k, t : t + 1, :]) for k in range(3)] for t in range(first, 8)]
    sums = [[None] * 6 for _ in range(far)]
    for g in range(BLK // 8):
        part = slice(8 * g, 8 * g + 8)
        here = [centre[n, k, part, :] for k in range(3)]
        cp = press[n, part, :]
        for t in range(far):
            row = 8 * (g * far + t)
            weight = outside[n, row : row + 8, :]
            for k in range(3):
                push = weight * (here[k] - ghost[t][k])
                for place, value in ((k, push * cp), (3 + k, push)):
                    old = sums[t][place]
                    sums[t][place] = value if old is None else old + value
    for t in range(far):
        for k in range(6):
            row = 8 * (k * far + t)
            others[n, row : row + 8, :] = sums[t][k]


def make_density_kernel(peers, slots):
    def density_kernel(own, before, codes, ids, counts, far, exports, *refs):
        sent = by_partner(refs[:peers])
        near, density, centre, press, inside, outside = refs[peers : peers + 6]
        outs = refs[peers + 6 : 2 * peers + 6]
        (late_three, ghosts, first, second, sums, fresh, others, rows, back, *small) = refs[
            2 * peers + 6 :
        ]
        copies = fetch([ids, counts, far, exports], small[:4], small[4])
        ids, counts, far, exports = small[:4]
        count = late_three.shape[2] // BLK
        blocks = density.shape[0]
        me = lax.axis_index("gy")

        for q in range(peers):
            tables = tables_of(sent[q ^ 2], count)
            for c in range(count):
                values = sent[q][:, chunk(count + c)]
                code = wide(values[7:8, :]).astype(I32)
                late_three[q, :, chunk(c)] = patch(values, code, tables)

        def settle(values, q):
            code = wide(values[7:8, :]).astype(I32)
            tables = tables_of(sent[q ^ 2], count)
            tables += [late_three[q ^ 1, :, chunk(c)] for c in range(count)]
            return patch(values, code, tables)

        for q in range(peers):
            for t in range(slots):
                ghosts[:, chunk(q * slots + t)] = settle(sent[q][:, chunk(2 * count + t)], q)

        later = [sent[2][6:7, chunk(c)] for c in range(count)]
        later = [wide(x) for x in later + [late_three[1, 6:7, chunk(c)] for c in range(count)]]
        for v in range(blocks // 8):
            part = slice(8 * v, 8 * v + 8)
            density[part, :] = patch(before[part, :], codes[1, part, :], later)
        back[...] = jnp.zeros_like(back)

        for copy in copies:
            copy.wait()
        live = counts[0, 0] + counts[0, 1]
        nact = ids.shape[2]
        inner = own.shape[1]
        ngh = far.shape[3]

        def far_of(n):
            which, i = live_slot(counts, n, nact)
            return [far[0, which, i, t] ^ (me * slots) for t in range(ngh)]

        for n in range(TOTACT):
            for t in range(inner):
                near[n, :, t, :] = settle(own[n, t], 0)
            for t, g in enumerate(far_of(n)):
                near[n, :, inner + t, :] = ghosts[:, lanes(g)]

        def prepare(n, buffer):
            spread([near[n, k, 0:1, :] for k in range(5)], buffer, centre.at[n])

        prepare(0, first)

        def step(p, _):
            n = 2 * p
            prepare(n + 1, second)
            pair_sums(near, n, first, sums, inside, outside)
            prepare(jnp.minimum(n + 2, TOTACT - 1), first)
            pair_sums(near, n + 1, second, sums, inside, outside)
            return 0

        lax.fori_loop(0, (live + 1) // 2, step, 0)
        for n in range(TOTACT):
            h = near[n, 4, 0:1, :]
            total = jnp.sum(jnp.transpose(sums[n]), axis=0, keepdims=True)
            fresh[n : n + 1, :] = total * (4.0 * KERNEL_NORM / (h * h * h))
        pressures = [near[n, 5, 0:1, :] / fresh[n : n + 1, :] for n in range(TOTACT)]
        pressures = jnp.concatenate(pressures + pressures[: 16 - TOTACT], axis=0)
        pressures = jnp.transpose(pressures)
        for n in range(TOTACT):
            press[n] = jnp.broadcast_to(pressures[:, n : n + 1], (BLK, BLK))

        def back_step(n, _):
            back_sums(near, n, centre, press, outside, others)
            which, i = live_slot(counts, n, nact)
            density[pl.ds(ids[0, which, i], 1), :] = fresh[pl.ds(n, 1), :]
            return 0

        lax.fori_loop(0, live, back_step, 0)
        for n in range(TOTACT):
            for t in range(ngh):
                m = near[n, 3, inner + t : inner + t + 1, :]
                u = near[n, 5, inner + t : inner + t + 1, :]
                scale = -FORCE_NORM / m
                for k in range(6):
                    row = 8 * (k * ngh + t)
                    total = jnp.sum(others[n, row : row + 8, :], axis=0, keepdims=True)
                    rows[n, k, t : t + 1, :] = total * (scale if k < 3 else scale * u)

        def place(n, _):
            for t, g in enumerate(far_of(n)):
                back[0:6, lanes(g)] += rows[n, 0:6, t, :]
            return 0

        lax.fori_loop(0, live, place, 0)
        for q in range(peers):
            outs[q][...] = back[:, q * slots * BLK : (q + 1) * slots * BLK]
            for t in range(slots):
                rho = density[pl.ds(exports[0, me ^ q, t], 1), :]
                outs[q][6:7, chunk(t)] = rho

    return density_kernel


def inner_sums(near, n, centre, press, others_press, inside, sums, others):
    local = inside.shape[1] // BLK
    tile = [[wide(near[n, k, t : t + 1, :]) for k in range(3)] for t in range(local)]
    theirs = [wide(others_press[n, t : t + 1, :]) for t in range(local)]
    pushed = [[None] * 3 for _ in range(local)]
    for g in range(BLK // 8):
        part = slice(8 * g, 8 * g + 8)
        here = [centre[n, k, part, :] for k in range(3)]
        cp = press[n, part, :]
        total = [None] * 3
        for t in range(local):
            row = 8 * (g * local + t)
            weight = inside[n, row : row + 8, :] * (cp + theirs[t])
            for k in range(3):
                push = weight * (here[k] - tile[t][k])
                total[k] = push if total[k] is None else total[k] + push
                if t > 0:
                    old = pushed[t][k]
                    pushed[t][k] = push if old is None else old + push
        for k in range(3):
            sums[n, k, part, :] = total[k]
    for t in range(1, local):
        for k in range(3):
            row = 8 * (k * local + t)
            others[n, row : row + 8, :] = pushed[t][k]


def inner_kernel(
    near, density, centre, press, inside, ids, counts, nbrs, totals, sums, density_out, *refs
):
    rho, others_press, others, rows = refs
    density_out[...] = density[...]
    totals[...] = jnp.zeros_like(totals)
    live = counts[0, 0] + counts[0, 1]
    nact = ids.shape[2]
    inner = 1 + nbrs.shape[3]

    def blocks_of(n):
        which, i = live_slot(counts, n, nact)
        return [ids[0, which, i]] + [nbrs[0, which, i, t] for t in range(nbrs.shape[3])]

    for n in range(TOTACT):
        for t, block in enumerate(blocks_of(n)):
            rho[n, t : t + 1, :] = density[pl.ds(block, 1), :]
    for n in range(TOTACT):
        others_press[n] = near[n, 5] / rho[n]

    def step(n, _):
        inner_sums(near, n, centre, press, others_press, inside, sums, others)
        return 0

    lax.fori_loop(0, live, step, 0)
    for n in range(TOTACT):
        for t in range(1, inner):
            scale = -FORCE_NORM / near[n, 3, t : t + 1, :]
            for k in range(3):
                row = 8 * (k * inner + t)
                total = jnp.sum(others[n, row : row + 8, :], axis=0, keepdims=True)
                rows[n, k, t : t + 1, :] = total * scale

    def place(n, _):
        for t, block in enumerate(blocks_of(n)):
            if t > 0:
                totals[0:3, lanes(block)] += rows[n, 0:3, t, :]
        return 0

    lax.fori_loop(0, live, place, 0)


def outer_sums(near, n, centre, press, others_press, outside, before, sums):
    far = outside.shape[1] // BLK
    first = 8 - far
    tile = [[wide(near[n, k, t : t + 1, :]) for k in range(3)] for t in range(first, 8)]
    theirs = [wide(others_press[n, t : t + 1, :]) for t in range(first, 8)]
    for g in range(BLK // 8):
        part = slice(8 * g, 8 * g + 8)
        here = [centre[n, k, part, :] for k in range(3)]
        cp = press[n, part, :]
        total = [before[n, k, part, :] for k in range(3)]
        for t in range(far):
            row = 8 * (g * far + t)
            weight = outside[n, row : row + 8, :] * (cp + theirs[t])
            for k in range(3):
                total[k] = total[k] + weight * (here[k] - tile[t][k])
        for k in range(3):
            sums[n, k, part, :] = total[k]


def make_outer_kernel(peers, slots):
    def outer_kernel(
        near, density, centre, press, outside, totals, before, ids, counts, far, exports, *refs
    ):
        got = by_partner(refs[:peers])
        out, far_rho, rho, others_press, sums, rows, *small = refs[peers:]
        copies = fetch([ids, counts, far, exports], small[:4], small[4])
        ids, counts, far, exports = small[:4]
        for q in range(peers):
            for t in range(slots):
                g = q * slots + t
                far_rho[g : g + 1, :] = got[q][6:7, chunk(t)]
        out[...] = totals[0:3, :]
        me = lax.axis_index("gy")
        nact = ids.shape[2]
        ngh = far.shape[3]
        for copy in copies:
            copy.wait()
        live = counts[0, 0] + counts[0, 1]
        for n in range(TOTACT):
            which, i = live_slot(counts, n, nact)
            for t in range(ngh):
                g = far[0, which, i, t] ^ (me * slots)
                rho[n, 8 - ngh + t : 9 - ngh + t, :] = far_rho[pl.ds(g, 1), :]
        for n in range(TOTACT):
            others_press[n] = near[n, 5] / rho[n]

        def step(n, _):
            outer_sums(near, n, centre, press, others_press, outside, before, sums)
            return 0

        lax.fori_loop(0, live, step, 0)
        for n in range(TOTACT):
            scale = FORCE_NORM / near[n, 3, 0:1, :]
            for k in range(3):
                total = jnp.sum(jnp.transpose(sums[n, k]), axis=0, keepdims=True)
                rows[n, k : k + 1, :] = total * scale
        for q in range(peers):
            for t in range(slots):
                b = exports[0, me ^ q, t]
                own_rho = density[pl.ds(b, 1), :]
                value = got[q][0:3, chunk(t)] + got[q][3:6, chunk(t)] / own_rho
                out[0:3, lanes(b)] += value

        def place(n, _):
            which, i = live_slot(counts, n, nact)
            out[0:3, lanes(ids[0, which, i])] += rows[n, 0:3, :]
            return 0

        lax.fori_loop(0, live, place, 0)

    return outer_kernel


def crossed(block, axis, bits):
    size = lax.axis_size(axis)
    return lax.ppermute(block, axis, [(i, i ^ bits) for i in range(size) if i ^ bits < size])


def exchanged(parts):
    return [parts[0]] + [crossed(parts[q], "gy", q) for q in range(len(parts) - 1, 0, -1)]


def by_partner(refs):
    return [refs[0]] + list(refs[:0:-1])


def shards(
    particles, mig_count, mig_rows, active_ids, active_count, local_nbrs, ghost_slots, export_blocks
):
    peers = lax.axis_size("gy")
    slots = export_blocks.shape[2]
    per_dev = particles.shape[1]
    blocks = per_dev // BLK
    mig = mig_rows.shape[2]
    inner = 1 + local_nbrs.shape[3]
    wide_total = peers * slots * BLK

    ints = jnp.concatenate(
        [
            mig_rows[0],
            jnp.pad(mig_count, ((0, 3), (0, mig - 4))),
            jnp.pad(export_blocks[0], ((0, 0), (0, mig - slots))),
        ],
        axis=0,
    )
    sent0, state = call(first_kernel, [shape(8, mig), shape(8, per_dev)], particles, ints)
    codes = call(codes_kernel, shape(4, blocks, BLK, dtype=I32), ints)
    got0 = crossed(sent0, "gx", 2)
    cols1, marks1, tables = call(
        early_tables_kernel,
        [shape(8, mig), shape(8, mig, dtype=I32), shape(4, blocks, BLK, dtype=I32)],
        state,
        ints,
        codes,
    )
    sent1 = call(second_kernel, shape(8, mig), cols1, marks1, got0)
    got1 = crossed(sent1, "gx", 1)
    cols, marks, raw, code_rows = call(
        late_tables_kernel,
        [
            shape(2, 8, mig),
            shape(8, mig, dtype=I32),
            shape(8, wide_total),
            shape(peers, slots, BLK, dtype=I32),
        ],
        state,
        ints,
        tables,
        sent1,
        scratch=[SMEM((peers, BLK), I32), DMA((1,))],
    )
    packs = call(
        export_kernel,
        [shape(8, 2 * mig + slots * BLK)] * peers,
        cols,
        marks,
        got0,
        got1,
        raw,
        code_rows,
    )
    sent = exchanged(packs)
    own, before = call(
        own_kernel,
        [shape(TOTACT, inner, 8, BLK), shape(blocks, BLK)],
        state,
        got0,
        got1,
        tables,
        active_ids,
        active_count,
        local_nbrs,
        smem=(4, 5, 6),
    )
    indices = [active_ids, active_count, ghost_slots, export_blocks]
    local = shape(TOTACT, inner * BLK, BLK)
    remote = shape(TOTACT, (8 - inner) * BLK, BLK)
    near, density, centre, press, inside, outside, *returns = call(
        make_density_kernel(peers, slots),
        [
            shape(TOTACT, 8, 8, BLK),
            shape(blocks, BLK),
            shape(TOTACT, 5, BLK, BLK),
            shape(TOTACT, BLK, BLK),
            local,
            remote,
        ]
        + [shape(8, slots * BLK)] * peers,
        own,
        before,
        tables,
        *indices,
        *sent,
        scratch=[
            VMEM((peers, 8, mig), F32),
            VMEM((8, wide_total), F32),
            VMEM((5, BLK, BLK), F32),
            VMEM((5, BLK, BLK), F32),
            VMEM((TOTACT, BLK, BLK), F32),
            VMEM((TOTACT, BLK), F32),
            VMEM((TOTACT, 6 * (8 - inner) * 8, BLK), F32),
            VMEM((TOTACT, 8, 8, BLK), F32),
            VMEM((8, wide_total), F32),
        ]
        + fetch_scratch(indices),
    )
    got = exchanged(returns)
    totals, sums, density_out = call(
        inner_kernel,
        [shape(8, per_dev), shape(TOTACT, 3, BLK, BLK), shape(blocks, BLK)],
        near,
        density,
        centre,
        press,
        inside,
        active_ids,
        active_count,
        local_nbrs,
        smem=(5, 6, 7),
        scratch=[
            VMEM((TOTACT, 8, BLK), F32),
            VMEM((TOTACT, 8, BLK), F32),
            VMEM((TOTACT, 3 * inner * 8, BLK), F32),
            VMEM((TOTACT, 8, 8, BLK), F32),
        ],
    )
    accel = call(
        make_outer_kernel(peers, slots),
        shape(3, per_dev),
        near,
        density,
        centre,
        press,
        outside,
        totals,
        sums,
        *indices,
        *got,
        scratch=[
            VMEM((peers * slots, BLK), F32),
            VMEM((TOTACT, 8, BLK), F32),
            VMEM((TOTACT, 8, BLK), F32),
            VMEM((TOTACT, 3, BLK, BLK), F32),
            VMEM((TOTACT, 8, BLK), F32),
        ]
        + fetch_scratch(indices),
    )
    return density_out.reshape(-1), accel


def solution(mesh):
    both = ("gx", "gy")
    placed = (
        P(None, both),
        P(both, None),
        P(both, None, None),
        P(both, None, None),
        P(both, None),
        P(both, None, None, None),
        P(both, None, None, None),
        P(both, None, None),
    )
    return jax.shard_map(
        shards,
        mesh=mesh,
        in_specs=placed,
        out_specs=(P(both), P(None, both)),
        check_vma=False,
    )
```

```python
import math

import jax
import jax.numpy as jnp
from jax import lax
from jax.experimental import pallas as pl
from jax.experimental.pallas import tpu as pltpu
from jax.sharding import PartitionSpec as P

BLK = 128
TOTACT = 12
KERNEL_NORM = 21.0 / (16.0 * math.pi)
FORCE_NORM = 5.0 * KERNEL_NORM * 32.0 * (2.0 / 3.0)
TINY = 1e-30
BLOCK_ORDER = (3, 1, 2)
RETURN_ORDER = (2, 3, 1)
F32 = jnp.float32
I32 = jnp.int32
VMEM = pltpu.VMEM
SMEM = pltpu.SMEM
DMA = pltpu.SemaphoreType.DMA


def call(kernel, out_shape, *args, smem=(), scratch=(), limit=16 << 20, cost=0):
    def space(n):
        return SMEM if n in smem else VMEM

    return pl.pallas_call(
        kernel,
        out_shape=out_shape,
        in_specs=[pl.BlockSpec(memory_space=space(n)) for n in range(len(args))],
        out_specs=jax.tree.map(lambda _: pl.BlockSpec(memory_space=VMEM), out_shape),
        scratch_shapes=list(scratch),
        compiler_params=pltpu.CompilerParams(vmem_limit_bytes=limit),
        cost_estimate=pl.CostEstimate(flops=0, transcendentals=0, bytes_accessed=cost)
        if cost
        else None,
    )(*args)


def shape(*dims, dtype=F32):
    return jax.ShapeDtypeStruct(dims, dtype)


def wide(row):
    return jnp.broadcast_to(row, (8, BLK))


def lanes(block):
    return pl.ds(pl.multiple_of(block * BLK, BLK), BLK)


def chunk(c):
    return slice(c * BLK, (c + 1) * BLK)


def take(values, index):
    return jnp.take_along_axis(values, index, axis=1)


def patch(values, code, tables):
    lane = code & (BLK - 1)
    which = code >> 7
    for n, table in enumerate(tables):
        values = jnp.where(which == n, take(table, lane), values)
    return values


def tables_of(ref, count, start=0):
    return [ref[:, chunk(start + c)] for c in range(count)]


def columns(state, slots):
    block = slots >> 7
    lane = slots & (BLK - 1)
    found = jnp.zeros((8, BLK), F32)
    for b in range(state.shape[1] // BLK):
        found = jnp.where(block == b, take(state[:, chunk(b)], lane), found)
    return found


def fetch(sources, targets, sems):
    copies = [
        pltpu.make_async_copy(a, b, sems.at[n]) for n, (a, b) in enumerate(zip(sources, targets))
    ]
    for copy in copies:
        copy.start()
    return copies


def fetch_scratch(arrays):
    return [SMEM(a.shape, I32) for a in arrays] + [DMA((len(arrays),))]


def first_kernel(particles, ints, out, state):
    state[0:7, :] = particles[...]
    state[7:8, :] = jnp.zeros((1, state.shape[1]), F32)
    for c in range(ints.shape[1] // BLK):
        out[:, chunk(c)] = columns(state, wide(ints[0:1, chunk(c)]))


def code_table(ints, level, blocks):
    mig = ints.shape[1]
    slots = ints[level : level + 1, :]
    k = lax.broadcasted_iota(I32, (1, mig), 1)
    low = (k & (BLK - 1)).astype(F32)
    high = ((k >> 7) + 1).astype(F32)
    in_block = lax.broadcasted_iota(I32, (blocks, mig), 0) == (slots >> 7)
    in_lane = lax.broadcasted_iota(I32, (BLK, mig), 0) == (slots & (BLK - 1))
    left = jnp.concatenate([jnp.where(in_block, low, 0.0), jnp.where(in_block, high, 0.0)], axis=0)
    right = jnp.where(in_lane, 1.0, 0.0)
    both = lax.dot_general(
        left.astype(jnp.bfloat16),
        right.astype(jnp.bfloat16),
        (((1,), (1,)), ((), ())),
        preferred_element_type=F32,
    )
    low, high = both[:blocks], both[blocks:]
    return jnp.where(high > 0.5, (high - 1.0) * BLK + low, -1.0).astype(I32)


def codes_kernel(ints, codes):
    for level in range(4):
        codes[level] = code_table(ints, level, codes.shape[1])


def code_at(table, slots):
    block = slots >> 7
    lane = slots & (BLK - 1)
    row = lax.broadcasted_iota(I32, (8, BLK), 0)
    found = jnp.full((8, BLK), -1, I32)
    for v in range(table.shape[0] // 8):
        piece = take(table[8 * v : 8 * v + 8, :], lane)
        found = jnp.where(block == row + 8 * v, piece, found)
    return jnp.max(found, axis=0, keepdims=True)


def early_tables_kernel(state, ints, codes, cols, marks, tables):
    mig = ints.shape[1]
    valid = []
    for level in range(4):
        code = codes[level]
        valid.append(jnp.where(code < ints[4:5, level : level + 1], code, -1))
    tables[0] = jnp.where(valid[1] >= 0, valid[1] + mig, valid[0])
    tables[1] = jnp.where(valid[3] >= 0, valid[3] + mig, valid[2])
    tables[2] = valid[2]
    tables[3] = valid[0]
    for c in range(mig // BLK):
        slots = wide(ints[1:2, chunk(c)])
        marks[0:1, chunk(c)] = code_at(tables.at[3], slots)
        cols[:, chunk(c)] = columns(state, slots)


def late_tables_kernel(
    state, ints, tables, after, cols, marks, raw, code_rows, exported, sems
):
    peers, slots, _ = code_rows.shape
    copies = fetch([ints.at[pl.ds(8, peers), pl.ds(0, BLK)]], [exported], sems)
    for c in range(ints.shape[1] // BLK):
        two, three = (wide(ints[level : level + 1, chunk(c)]) for level in (2, 3))
        marks[1:2, chunk(c)] = code_at(tables.at[0], two)
        marks[2:3, chunk(c)] = code_at(tables.at[0], three)
        marks[3:4, chunk(c)] = code_at(tables.at[2], three)
        cols[0, :, chunk(c)] = columns(state, two)
        cols[1, :, chunk(c)] = columns(state, three)
    for copy in copies:
        copy.wait()
    me = lax.axis_index("gy")
    row = lax.broadcasted_iota(I32, (8, BLK), 0)
    for q in range(peers):
        for t in range(slots):
            block = exported[me ^ q, t]
            code = wide(tables[1, pl.ds(block, 1), :]).astype(F32)
            raw[:, chunk(q * slots + t)] = jnp.where(row == 7, code, state[:, lanes(block)])
            code_rows[q, t : t + 1, :] = tables[0, pl.ds(block, 1), :]


def second_kernel(cols, marks, got0, out):
    count = got0.shape[1] // BLK
    tables = tables_of(got0, count)
    for c in range(count):
        out[:, chunk(c)] = patch(cols[:, chunk(c)], wide(marks[0:1, chunk(c)]), tables)


def early_block(state, codes, tables, block):
    row = lax.broadcasted_iota(I32, (8, BLK), 0)
    patched = patch(state[:, lanes(block)], wide(codes[0, pl.ds(block, 1), :]), tables)
    return jnp.where(row == 7, wide(codes[1, pl.ds(block, 1), :]).astype(F32), patched)


def export_kernel(cols, marks, got0, got1, raw, code_rows, *outs):
    count = got0.shape[1] // BLK
    slots = code_rows.shape[1]
    tables = tables_of(got0, count) + tables_of(got1, count)
    row = lax.broadcasted_iota(I32, (8, BLK), 0)
    for c in range(count):
        two = patch(cols[0, :, chunk(c)], wide(marks[1:2, chunk(c)]), tables)
        three = patch(cols[1, :, chunk(c)], wide(marks[2:3, chunk(c)]), tables)
        three = jnp.where(row == 7, wide(marks[3:4, chunk(c)]).astype(F32), three)
        for out in outs:
            out[:, chunk(c)] = two
            out[:, chunk(count + c)] = three
    for q, out in enumerate(outs):
        for t in range(slots):
            values = raw[:, chunk(q * slots + t)]
            patched = patch(values, wide(code_rows[q, t : t + 1, :]), tables)
            out[:, chunk(2 * count + t)] = jnp.where(row == 7, values, patched)


def live_slot(counts, n, nact):
    second = n >= counts[0, 0]
    return jnp.where(second, 1, 0), jnp.where(second, jnp.minimum(n - counts[0, 0], nact - 1), n)


def picked_rows(chosen, table):
    high = table.astype(jnp.bfloat16)
    rest = table - high.astype(F32)
    middle = rest.astype(jnp.bfloat16)
    low = (rest - middle.astype(F32)).astype(jnp.bfloat16)
    chosen = chosen.astype(jnp.bfloat16)
    return jnp.dot(
        jnp.concatenate([chosen] * 3, axis=1),
        jnp.concatenate([high, middle, low], axis=0),
        preferred_element_type=F32,
    )


def own_kernel(state, got0, got1, codes, ids, counts, nbrs, far, exports, *refs):
    own, density, near_pick, far_pick = refs[:4]
    copied, small = refs[4:9], refs[9:]
    for source, target in zip((ids, counts, nbrs, far, exports), copied):
        target[...] = source[...]
    copies = fetch([ids, counts, nbrs, far], small[:4], small[4])
    ids, counts, nbrs, far = small[:4]
    me = lax.axis_index("gy")
    slots = 8
    near_pick[...] = jnp.zeros_like(near_pick)
    far_pick[...] = jnp.zeros_like(far_pick)
    near_lane = lax.broadcasted_iota(I32, (1, near_pick.shape[1]), 1)
    far_lane = lax.broadcasted_iota(I32, (1, far_pick.shape[1]), 1)
    count = got0.shape[1] // BLK
    blocks = density.shape[0]
    tables = tables_of(got0, count) + tables_of(got1, count)
    last = [wide(table[6:7, :]) for table in tables]
    for b in range(blocks):
        density[b : b + 1, :] = state[6:7, chunk(b)]
    for v in range(blocks // 8):
        part = slice(8 * v, 8 * v + 8)
        density[part, :] = patch(density[part, :], codes[0, part, :], last)
    nact = ids.shape[2]

    for copy in copies:
        copy.wait()
    for n in range(TOTACT):
        which, i = live_slot(counts, n, nact)
        wanted = [ids[0, which, i]] + [nbrs[0, which, i, t] for t in range(nbrs.shape[3])]
        for t, block in enumerate(wanted):
            own[n, t] = early_block(state, codes, tables, block)
            near_pick[8 * n + t : 8 * n + t + 1, :] = jnp.where(near_lane == block, 1.0, 0.0)
        for t in range(far.shape[3]):
            g = far[0, which, i, t] ^ (me * slots)
            at = 8 * n + len(wanted) + t
            far_pick[at : at + 1, :] = jnp.where(far_lane == g, 1.0, 0.0)


def spread(rows, out, kept):
    columns_of = jnp.transpose(jnp.concatenate((rows + rows)[:8], axis=0))
    for k in range(len(rows)):
        values = jnp.broadcast_to(columns_of[:, k : k + 1], (BLK, BLK))
        out[k] = values
        if k < 5:
            kept[k] = values


def added(old, value):
    return value if old is None else old + value


def pair_weight(distance, h1, h2, m1, m2):
    inverse = 1.0 / (h1 + h2)
    inv2 = inverse * inverse
    slope = jnp.maximum(inverse - distance * inv2, 0.0)
    return slope * slope * slope * inv2 * (m1 * m2)


def pair_sums(near, n, centre, inside, outside, press, fresh, others):
    local = inside.shape[1] // BLK
    far = 8 - local
    row = lax.broadcasted_iota(I32, (8, BLK), 0)
    lane = lax.broadcasted_iota(I32, (8, BLK), 1)
    plain = [[None] * 3 for _ in range(far)]
    pressed = [[None] * 3 for _ in range(far)]
    own = None
    waiting = None

    def settle_pushes(pushes, pressure):
        for t in range(far):
            for k in range(3):
                pressed[t][k] = added(pressed[t][k], pushes[t][k] * pressure)

    for g in range(BLK // 8):
        part = slice(8 * g, 8 * g + 8)
        cx, cy, cz, cm, ch, cu = (centre[k, part, :] for k in range(6))
        half = 0.5 / ch
        total = None
        pushes = []
        for t in range(8):
            x, y, z, m, h = (wide(near[n, k, t : t + 1, :]) for k in range(5))
            apart = (cx - x, cy - y, cz - z)
            square = apart[0] * apart[0] + apart[1] * apart[1] + apart[2] * apart[2]
            distance = square * lax.rsqrt(jnp.maximum(square, TINY))
            fall = jnp.maximum(1.0 - distance * half, 0.0)
            fall2 = fall * fall
            total = added(total, fall2 * fall2 * (1.25 - fall) * m)
            if t < local:
                at = 8 * (g * local + t)
                inside[n, at : at + 8, :] = distance
            else:
                weight = pair_weight(distance, ch, h, cm, m)
                at = 8 * (g * far + t - local)
                push = [weight * apart[k] for k in range(3)]
                for k in range(3):
                    outside[n, k, at : at + 8, :] = push[k]
                    plain[t - local][k] = added(plain[t - local][k], push[k])
                pushes.append(push)
        total = jnp.broadcast_to(jnp.sum(total, axis=1, keepdims=True), (8, BLK))
        rho = total * (4.0 * KERNEL_NORM / (ch * ch * ch))
        pressure = cu / rho
        press[n, part, :] = pressure
        own = added(own, jnp.where(row + 8 * g == lane, rho, 0.0))
        if waiting is not None:
            settle_pushes(*waiting)
        waiting = (pushes, pressure)
    settle_pushes(*waiting)
    fresh[pl.ds(n, 1), :] = jnp.sum(own, axis=0, keepdims=True)
    for t in range(far):
        for k in range(3):
            at = 8 * (k * far + t)
            others[n, at : at + 8, :] = pressed[t][k]
            at = 8 * ((3 + k) * far + t)
            others[n, at : at + 8, :] = plain[t][k]


def make_density_kernel(peers, slots):
    def density_kernel(own, before, codes, ids, counts, far, exports, *refs):
        sent = by_partner(refs[:peers], BLOCK_ORDER)
        near, density, centre, press, inside, outside = refs[peers : peers + 6]
        outs = refs[peers + 6 : 2 * peers + 6]
        (late_three, ghosts, first, second, fresh, others, rows, back, *small) = refs[
            2 * peers + 6 :
        ]
        copies = fetch([ids, counts, far, exports], small[:4], small[4])
        ids, counts, far, exports = small[:4]
        count = late_three.shape[2] // BLK
        blocks = density.shape[0]
        me = lax.axis_index("gy")

        for q in range(peers):
            tables = tables_of(sent[q ^ 2], count)
            for c in range(count):
                values = sent[q][:, chunk(count + c)]
                code = wide(values[7:8, :]).astype(I32)
                late_three[q, :, chunk(c)] = patch(values, code, tables)

        def settle(values, q):
            code = wide(values[7:8, :]).astype(I32)
            tables = tables_of(sent[q ^ 2], count)
            tables += [late_three[q ^ 1, :, chunk(c)] for c in range(count)]
            return patch(values, code, tables)

        for q in range(peers):
            for t in range(slots):
                ghosts[:, chunk(q * slots + t)] = settle(sent[q][:, chunk(2 * count + t)], q)

        later = [sent[2][6:7, chunk(c)] for c in range(count)]
        later = [wide(x) for x in later + [late_three[1, 6:7, chunk(c)] for c in range(count)]]
        for v in range(blocks // 8):
            part = slice(8 * v, 8 * v + 8)
            density[part, :] = patch(before[part, :], codes[1, part, :], later)
        back[...] = jnp.zeros_like(back)

        for copy in copies:
            copy.wait()
        live = counts[0, 0] + counts[0, 1]
        nact = ids.shape[2]
        inner = own.shape[1]
        ngh = far.shape[3]

        def far_of(n):
            which, i = live_slot(counts, n, nact)
            return [far[0, which, i, t] ^ (me * slots) for t in range(ngh)]

        for n in range(TOTACT):
            for t in range(inner):
                near[n, :, t, :] = settle(own[n, t], 0)
            for t, g in enumerate(far_of(n)):
                near[n, :, inner + t, :] = ghosts[:, lanes(g)]

        def prepare(n, buffer):
            spread([near[n, k, 0:1, :] for k in range(6)], buffer, centre.at[n])

        def work(n, buffer):
            pair_sums(near, n, buffer, inside, outside, press, fresh, others)

        prepare(0, first)

        def step(p, _):
            n = 2 * p
            prepare(n + 1, second)
            work(n, first)
            prepare(jnp.minimum(n + 2, TOTACT - 1), first)
            work(n + 1, second)
            return 0

        lax.fori_loop(0, (live + 1) // 2, step, 0)
        for n in range(TOTACT):
            for t in range(ngh):
                m = near[n, 3, inner + t : inner + t + 1, :]
                u = near[n, 5, inner + t : inner + t + 1, :]
                scale = -FORCE_NORM / m
                for k in range(6):
                    row = 8 * (k * ngh + t)
                    total = jnp.sum(others[n, row : row + 8, :], axis=0, keepdims=True)
                    rows[n, k, t : t + 1, :] = total * (scale if k < 3 else scale * u)

        for n in range(TOTACT):
            for t, g in enumerate(far_of(n)):
                back[0:6, lanes(g)] += jnp.where(n < live, rows[n, 0:6, t, :], 0.0)

        def place(n, _):
            which, i = live_slot(counts, n, nact)
            density[pl.ds(ids[0, which, i], 1), :] = fresh[pl.ds(n, 1), :]
            return 0

        lax.fori_loop(0, live, place, 0)
        for q in range(peers):
            outs[q][...] = back[:, q * slots * BLK : (q + 1) * slots * BLK]
            for t in range(slots):
                rho = density[pl.ds(exports[0, me ^ q, t], 1), :]
                outs[q][6:7, chunk(t)] = rho

    return density_kernel


def inner_sums(near, n, centre, press, others_press, inside, sums, others):
    local = inside.shape[1] // BLK
    pushed = [[None] * 3 for _ in range(local)]
    for g in range(BLK // 8):
        part = slice(8 * g, 8 * g + 8)
        *here, cm, ch = (centre[n, k, part, :] for k in range(5))
        cp = press[n, part, :]
        total = [None] * 3
        for t in range(local):
            *tile, m, h = (wide(near[n, k, t : t + 1, :]) for k in range(5))
            row = 8 * (g * local + t)
            weight = pair_weight(inside[n, row : row + 8, :], ch, h, cm, m)
            weight = weight * (cp + wide(others_press[n, t : t + 1, :]))
            for k in range(3):
                push = weight * (here[k] - tile[k])
                total[k] = push if total[k] is None else total[k] + push
                if t > 0:
                    old = pushed[t][k]
                    pushed[t][k] = push if old is None else old + push
        for k in range(3):
            sums[n, k, part, :] = total[k]
    for t in range(1, local):
        for k in range(3):
            row = 8 * (k * local + t)
            others[n, row : row + 8, :] = pushed[t][k]


def inner_kernel(
    near, density, centre, press, inside, near_pick, ids, counts, nbrs, totals, sums, *refs
):
    others_press, others, rows, *small = refs
    copies = fetch([ids, counts, nbrs], small[:3], small[3])
    ids, counts, nbrs = small[:3]
    totals[...] = jnp.zeros_like(totals)
    rho = picked_rows(near_pick[...], density[...])
    for n in range(TOTACT):
        others_press[n] = near[n, 5] / rho[8 * n : 8 * n + 8]

    def step(n, _):
        inner_sums(near, n, centre, press, others_press, inside, sums, others)
        return 0

    lax.fori_loop(0, TOTACT, step, 0)
    for copy in copies:
        copy.wait()
    live = counts[0, 0] + counts[0, 1]
    inner = 1 + nbrs.shape[3]
    for n in range(TOTACT):
        which, i = live_slot(counts, n, ids.shape[2])
        for t in range(1, inner):
            scale = -FORCE_NORM / near[n, 3, t : t + 1, :]
            for k in range(3):
                row = 8 * (k * inner + t)
                total = jnp.sum(others[n, row : row + 8, :], axis=0, keepdims=True)
                rows[n, k, t : t + 1, :] = total * scale
            block = nbrs[0, which, i, t - 1]
            totals[0:3, lanes(block)] += jnp.where(n < live, rows[n, 0:3, t, :], 0.0)


def outer_sums(near, n, press, others_press, outside, before, rows):
    far = outside.shape[2] // BLK
    theirs = [wide(others_press[n, t : t + 1, :]) for t in range(8 - far, 8)]
    row = lax.broadcasted_iota(I32, (8, BLK), 0)
    lane = lax.broadcasted_iota(I32, (8, BLK), 1)
    own = [None] * 3
    for g in range(BLK // 8):
        part = slice(8 * g, 8 * g + 8)
        cp = press[n, part, :]
        total = [before[n, k, part, :] for k in range(3)]
        for t in range(far):
            at = 8 * (g * far + t)
            both = cp + theirs[t]
            for k in range(3):
                total[k] = total[k] + both * outside[n, k, at : at + 8, :]
        for k in range(3):
            value = jnp.broadcast_to(jnp.sum(total[k], axis=1, keepdims=True), (8, BLK))
            own[k] = added(own[k], jnp.where(row + 8 * g == lane, value, 0.0))
    scale = FORCE_NORM / near[n, 3, 0:1, :]
    for k in range(3):
        rows[n, k : k + 1, :] = jnp.sum(own[k], axis=0, keepdims=True) * scale


def make_outer_kernel(peers, slots):
    def outer_kernel(
        near, density, press, outside, totals, before, far_pick, ids, counts, exports, *refs
    ):
        sent = refs[:peers]
        got = by_partner(refs[peers : 2 * peers], RETURN_ORDER)
        out, density_out, far_rho, others_press, rows, *small = refs[2 * peers :]
        copies = fetch([ids, counts, exports], small[:3], small[3])
        ids, counts, exports = small[:3]
        density_out[...] = density[...]
        far_rho[...] = jnp.zeros_like(far_rho)
        for q in range(peers):
            for t in range(slots):
                g = q * slots + t
                far_rho[g : g + 1, :] = got[q][6:7, chunk(t)]
        out[...] = totals[0:3, :]
        rho = picked_rows(far_pick[...], far_rho[...])
        for n in range(TOTACT):
            others_press[n] = near[n, 5] / rho[8 * n : 8 * n + 8]

        def step(n, _):
            outer_sums(near, n, press, others_press, outside, before, rows)
            return 0

        lax.fori_loop(0, TOTACT, step, 0)
        for copy in copies:
            copy.wait()
        me = lax.axis_index("gy")
        live = counts[0, 0] + counts[0, 1]
        for q in range(peers):
            for t in range(slots):
                own_rho = sent[q][6:7, chunk(t)]
                value = got[q][0:3, chunk(t)] + got[q][3:6, chunk(t)] / own_rho
                out[0:3, lanes(exports[0, me ^ q, t])] += value
        for n in range(TOTACT):
            which, i = live_slot(counts, n, ids.shape[2])
            out[0:3, lanes(ids[0, which, i])] += jnp.where(n < live, rows[n, 0:3, :], 0.0)

    return outer_kernel


def crossed(block, axis, bits):
    size = lax.axis_size(axis)
    return lax.ppermute(block, axis, [(i, i ^ bits) for i in range(size) if i ^ bits < size])


def first_steps(peers, first):
    return list(first) + [q for q in range(peers - 1, 0, -1) if q not in first]


def exchanged(parts, first):
    return [parts[0]] + [crossed(parts[q], "gy", q) for q in first_steps(len(parts), first)]


def by_partner(refs, first):
    steps = [0] + first_steps(len(refs), first)
    return [refs[steps.index(q)] for q in range(len(refs))]


def shards(
    particles, mig_count, mig_rows, active_ids, active_count, local_nbrs, ghost_slots, export_blocks
):
    peers = lax.axis_size("gy")
    slots = export_blocks.shape[2]
    per_dev = particles.shape[1]
    blocks = per_dev // BLK
    mig = mig_rows.shape[2]
    inner = 1 + local_nbrs.shape[3]
    wide_total = peers * slots * BLK

    ints = jnp.concatenate(
        [
            mig_rows[0],
            jnp.pad(mig_count, ((0, 3), (0, mig - 4))),
            jnp.pad(export_blocks[0], ((0, 0), (0, mig - slots))),
        ],
        axis=0,
    )
    sent0, state = call(first_kernel, [shape(8, mig), shape(8, per_dev)], particles, ints)
    codes = call(codes_kernel, shape(4, blocks, BLK, dtype=I32), ints)
    got0 = crossed(sent0, "gx", 2)
    cols1, marks1, tables = call(
        early_tables_kernel,
        [shape(8, mig), shape(8, mig, dtype=I32), shape(4, blocks, BLK, dtype=I32)],
        state,
        ints,
        codes,
    )
    sent1 = call(second_kernel, shape(8, mig), cols1, marks1, got0)
    got1 = crossed(sent1, "gx", 1)
    cols, marks, raw, code_rows = call(
        late_tables_kernel,
        [
            shape(2, 8, mig),
            shape(8, mig, dtype=I32),
            shape(8, wide_total),
            shape(peers, slots, BLK, dtype=I32),
        ],
        state,
        ints,
        tables,
        sent1,
        scratch=[SMEM((peers, BLK), I32), DMA((1,))],
    )
    packs = call(
        export_kernel,
        [shape(8, 2 * mig + slots * BLK)] * peers,
        cols,
        marks,
        got0,
        got1,
        raw,
        code_rows,
    )
    sent = exchanged(packs, BLOCK_ORDER)
    small = [active_ids, active_count, local_nbrs, ghost_slots]
    own, before, near_pick, far_pick, ids, counts, nbrs, far, export_ids = call(
        own_kernel,
        [
            shape(TOTACT, inner, 8, BLK),
            shape(blocks, BLK),
            shape(TOTACT * 8, blocks),
            shape(TOTACT * 8, max(BLK, peers * slots)),
        ]
        + [shape(*a.shape, dtype=I32) for a in small + [export_blocks]],
        state,
        got0,
        got1,
        tables,
        *small,
        export_blocks,
        scratch=fetch_scratch(small),
    )
    indices = [ids, counts, far, export_ids]
    local = shape(TOTACT, inner * BLK, BLK)
    remote = shape(TOTACT, 3, (8 - inner) * BLK, BLK)
    near, density, centre, press, inside, outside, *returns = call(
        make_density_kernel(peers, slots),
        [
            shape(TOTACT, 8, 8, BLK),
            shape(blocks, BLK),
            shape(TOTACT, 5, BLK, BLK),
            shape(TOTACT, BLK, BLK),
            local,
            remote,
        ]
        + [shape(8, slots * BLK)] * peers,
        own,
        before,
        tables,
        *indices,
        *sent,
        scratch=[
            VMEM((peers, 8, mig), F32),
            VMEM((8, wide_total), F32),
            VMEM((6, BLK, BLK), F32),
            VMEM((6, BLK, BLK), F32),
            VMEM((TOTACT, BLK), F32),
            VMEM((TOTACT, 6 * (8 - inner) * 8, BLK), F32),
            VMEM((TOTACT, 8, 8, BLK), F32),
            VMEM((8, wide_total), F32),
        ]
        + fetch_scratch(indices),
    )
    got = exchanged(returns, RETURN_ORDER)
    small = [ids, counts, nbrs]
    totals, sums = call(
        inner_kernel,
        [shape(8, per_dev), shape(TOTACT, 3, BLK, BLK)],
        near,
        density,
        centre,
        press,
        inside,
        near_pick,
        *small,
        scratch=[
            VMEM((TOTACT, 8, BLK), F32),
            VMEM((TOTACT, 3 * inner * 8, BLK), F32),
            VMEM((TOTACT, 8, 8, BLK), F32),
        ]
        + fetch_scratch(small),
    )
    small = [ids, counts, export_ids]
    accel, density_out = call(
        make_outer_kernel(peers, slots),
        [shape(3, per_dev), shape(blocks, BLK)],
        near,
        density,
        press,
        outside,
        totals,
        sums,
        far_pick,
        *small,
        *returns,
        *got,
        scratch=[
            VMEM((max(BLK, peers * slots), BLK), F32),
            VMEM((TOTACT, 8, BLK), F32),
            VMEM((TOTACT, 8, BLK), F32),
        ]
        + fetch_scratch(small),
    )
    return density_out.reshape(-1), accel


def solution(mesh):
    both = ("gx", "gy")
    placed = (
        P(None, both),
        P(both, None),
        P(both, None, None),
        P(both, None, None),
        P(both, None),
        P(both, None, None, None),
        P(both, None, None, None),
        P(both, None, None),
    )
    return jax.shard_map(
        shards,
        mesh=mesh,
        in_specs=placed,
        out_specs=(P(both), P(None, both)),
        check_vma=False,
    )
```

```python
import math

import jax
import jax.numpy as jnp
from jax import lax
from jax.experimental import pallas as pl
from jax.experimental.pallas import tpu as pltpu
from jax.sharding import PartitionSpec as P

BLK = 128
TOTACT = 12
KERNEL_NORM = 21.0 / (16.0 * math.pi)
FORCE_NORM = 5.0 * KERNEL_NORM * 32.0 * (2.0 / 3.0)
TINY = 1e-30
BLOCK_ORDER = (2, 3, 1)
RETURN_ORDER = (2, 3, 1)
PIECES = 4
F32 = jnp.float32
I32 = jnp.int32
VMEM = pltpu.VMEM
SMEM = pltpu.SMEM
DMA = pltpu.SemaphoreType.DMA


def call(kernel, out_shape, *args, smem=(), scratch=(), limit=16 << 20, out_any=False):
    def space(n):
        return SMEM if n in smem else VMEM

    return pl.pallas_call(
        kernel,
        out_shape=out_shape,
        in_specs=[pl.BlockSpec(memory_space=space(n)) for n in range(len(args))],
        out_specs=jax.tree.map(
            lambda _: pl.BlockSpec(memory_space=pl.ANY if out_any else VMEM), out_shape
        ),
        scratch_shapes=list(scratch),
        compiler_params=pltpu.CompilerParams(vmem_limit_bytes=limit),
    )(*args)


def shape(*dims, dtype=F32):
    return jax.ShapeDtypeStruct(dims, dtype)


def wide(row):
    return jnp.broadcast_to(row, (8, BLK))


def lanes(block):
    return pl.ds(pl.multiple_of(block * BLK, BLK), BLK)


def chunk(c):
    return slice(c * BLK, (c + 1) * BLK)


def take(values, index):
    return jnp.take_along_axis(values, index, axis=1)


def patch(values, code, tables):
    lane = code & (BLK - 1)
    which = code >> 7
    for n, table in enumerate(tables):
        values = jnp.where(which == n, take(table, lane), values)
    return values


def tables_of(ref, count, start=0):
    return [ref[:, chunk(start + c)] for c in range(count)]


def columns(state, slots):
    block = slots >> 7
    lane = slots & (BLK - 1)
    found = jnp.zeros((8, BLK), F32)
    for b in range(state.shape[1] // BLK):
        found = jnp.where(block == b, take(state[:, chunk(b)], lane), found)
    return found


def fetch(sources, targets, sems):
    copies = [
        pltpu.make_async_copy(a, b, sems.at[n]) for n, (a, b) in enumerate(zip(sources, targets))
    ]
    for copy in copies:
        copy.start()
    return copies


def fetch_scratch(arrays):
    return [SMEM(a.shape, I32) for a in arrays] + [DMA((len(arrays),))]


def first_kernel(state, ints, out):
    for c in range(ints.shape[1] // BLK):
        out[:, chunk(c)] = columns(state, wide(ints[0:1, chunk(c)]))


def code_table(ints, level, blocks):
    mig = ints.shape[1]
    slots = ints[level : level + 1, :]
    k = lax.broadcasted_iota(I32, (1, mig), 1)
    low = (k & (BLK - 1)).astype(F32)
    high = ((k >> 7) + 1).astype(F32)
    in_block = lax.broadcasted_iota(I32, (blocks, mig), 0) == (slots >> 7)
    in_lane = lax.broadcasted_iota(I32, (BLK, mig), 0) == (slots & (BLK - 1))
    left = jnp.concatenate([jnp.where(in_block, low, 0.0), jnp.where(in_block, high, 0.0)], axis=0)
    right = jnp.where(in_lane, 1.0, 0.0)
    both = lax.dot_general(
        left.astype(jnp.bfloat16),
        right.astype(jnp.bfloat16),
        (((1,), (1,)), ((), ())),
        preferred_element_type=F32,
    )
    low, high = both[:blocks], both[blocks:]
    return jnp.where(high > 0.5, (high - 1.0) * BLK + low, -1.0).astype(I32)


def codes_kernel(ints, codes):
    for level in range(4):
        codes[level] = code_table(ints, level, codes.shape[1])


def code_at(table, slots):
    block = slots >> 7
    lane = slots & (BLK - 1)
    row = lax.broadcasted_iota(I32, (8, BLK), 0)
    found = jnp.full((8, BLK), -1, I32)
    for v in range(table.shape[0] // 8):
        piece = take(table[8 * v : 8 * v + 8, :], lane)
        found = jnp.where(block == row + 8 * v, piece, found)
    return jnp.max(found, axis=0, keepdims=True)


def early_tables_kernel(state, ints, codes, cols, marks, tables):
    mig = ints.shape[1]
    valid = []
    for level in range(4):
        code = codes[level]
        valid.append(jnp.where(code < ints[4:5, level : level + 1], code, -1))
    tables[0] = jnp.where(valid[1] >= 0, valid[1] + mig, valid[0])
    tables[1] = jnp.where(valid[3] >= 0, valid[3] + mig, valid[2])
    tables[2] = valid[2]
    tables[3] = valid[0]
    for c in range(mig // BLK):
        slots = wide(ints[1:2, chunk(c)])
        two, three = (wide(ints[level : level + 1, chunk(c)]) for level in (2, 3))
        marks[0:1, chunk(c)] = code_at(tables.at[3], slots)
        marks[1:2, chunk(c)] = code_at(tables.at[0], two)
        marks[2:3, chunk(c)] = code_at(tables.at[0], three)
        marks[3:4, chunk(c)] = code_at(tables.at[2], three)
        cols[:, chunk(c)] = columns(state, slots)


def late_tables_kernel(
    state, ints, tables, after, cols, raw, code_rows, exported, sems
):
    peers, slots, _ = code_rows.shape
    copies = fetch([ints.at[pl.ds(8, peers), pl.ds(0, BLK)]], [exported], sems)
    for c in range(ints.shape[1] // BLK):
        two, three = (wide(ints[level : level + 1, chunk(c)]) for level in (2, 3))
        cols[0, :, chunk(c)] = columns(state, two)
        cols[1, :, chunk(c)] = columns(state, three)
    for copy in copies:
        copy.wait()
    me = lax.axis_index("gy")
    row = lax.broadcasted_iota(I32, (8, BLK), 0)
    for q in range(peers):
        for t in range(slots):
            block = exported[me ^ q, t]
            code = wide(tables[1, pl.ds(block, 1), :]).astype(F32)
            raw[:, chunk(q * slots + t)] = jnp.where(row == 7, code, state[:, lanes(block)])
            code_rows[q, t : t + 1, :] = tables[0, pl.ds(block, 1), :]


def second_kernel(cols, marks, got0, out):
    count = got0.shape[1] // BLK
    tables = tables_of(got0, count)
    for c in range(count):
        out[:, chunk(c)] = patch(cols[:, chunk(c)], wide(marks[0:1, chunk(c)]), tables)


def early_block(state, codes, tables, block):
    row = lax.broadcasted_iota(I32, (8, BLK), 0)
    patched = patch(state[:, lanes(block)], wide(codes[0, pl.ds(block, 1), :]), tables)
    return jnp.where(row == 7, wide(codes[1, pl.ds(block, 1), :]).astype(F32), patched)


def packed_width(mig, slots):
    total = mig * 2 // BLK + slots
    return total - total // 8


def export_kernel(cols, marks, got0, got1, raw, code_rows, *outs):
    count = got0.shape[1] // BLK
    slots = code_rows.shape[1]
    tables = tables_of(got0, count) + tables_of(got1, count)
    row = lax.broadcasted_iota(I32, (8, BLK), 0)
    twos, threes = [], []
    for c in range(count):
        twos.append(patch(cols[0, :, chunk(c)], wide(marks[1:2, chunk(c)]), tables))
        three = patch(cols[1, :, chunk(c)], wide(marks[2:3, chunk(c)]), tables)
        threes.append((three, wide(marks[3:4, chunk(c)]).astype(F32)))
    for q, out in enumerate(outs):
        coded = list(threes)
        for t in range(slots):
            values = raw[:, chunk(q * slots + t)]
            patched = patch(values, wide(code_rows[q, t : t + 1, :]), tables)
            coded.append((patched, wide(values[7:8, :])))
        code_row = 7 if q == 0 else 6
        items = list(twos)
        if q == 1:
            for c in range(count):
                items[c] = jnp.where(row == 6, wide(threes[c][0][6:7, :]), twos[c])
        items += [jnp.where(row == code_row, code, v) for v, code in coded]
        kept = out.shape[1] // BLK
        for i in range(kept):
            item = items[i]
            if kept < len(items):
                item = jnp.where(row == 7, wide(items[kept + i // 7][i % 7 : i % 7 + 1, :]), item)
            out[:, chunk(i)] = item


def unpacked(ref, total):
    kept = ref.shape[1] // BLK
    items = [ref[:, chunk(i)] for i in range(kept)]
    for extra in range(total - kept):
        rows = [ref[7:8, chunk(7 * extra + r)] for r in range(7)]
        items.append(jnp.concatenate(rows + rows[:1], axis=0))
    return items, 7 if kept == total else 6


class Indices:
    def __init__(self, ref, near, far):
        self.ref, self.near, self.far = ref, near, far
        self.counts = 2 + 2 * (near + far)

    def live(self):
        return self.ref[self.counts, 0] + self.ref[self.counts, 1]

    def slot(self, n):
        first = self.ref[self.counts, 0]
        second = n >= first
        last = self.ref.shape[1] - 1
        return jnp.where(second, 1, 0), jnp.where(second, jnp.minimum(n - first, last), n)

    def active(self, n):
        which, i = self.slot(n)
        return self.ref[which, i]

    def near_blocks(self, n):
        which, i = self.slot(n)
        return [self.ref[2 + 2 * t + which, i] for t in range(self.near)]

    def ghosts(self, n, mine):
        which, i = self.slot(n)
        start = 2 + 2 * self.near + which * self.far
        return [self.ref[start + t, i] ^ mine for t in range(self.far)]

    def exported(self, place, t):
        return self.ref[self.counts + 1 + place, t]


def pack_indices(packed, ids, counts, nbrs, far, exports):
    packed[...] = jnp.zeros_like(packed)
    packed[0:2, :] = ids[0]
    at = 2
    for part in (nbrs, far):
        for k in range(part.shape[1]):
            packed[at : at + part.shape[2], :] = part[0, k]
            at += part.shape[2]
    packed[at : at + 1, 0:2] = counts[...]
    packed[at + 1 : at + 1 + exports.shape[1], :] = exports[0]


def picked_rows(chosen, table):
    high = table.astype(jnp.bfloat16)
    rest = table - high.astype(F32)
    middle = rest.astype(jnp.bfloat16)
    low = (rest - middle.astype(F32)).astype(jnp.bfloat16)
    chosen = chosen.astype(jnp.bfloat16)
    return jnp.dot(
        jnp.concatenate([chosen] * 3, axis=1),
        jnp.concatenate([high, middle, low], axis=0),
        preferred_element_type=F32,
    )


def own_kernel(
    state, got0, got1, codes, ids, counts, nbrs, far, exports, own, density, near_pick, far_pick,
    packed, *small
):
    pack_indices(packed, ids, counts, nbrs, far, exports)
    copies = fetch([packed], [small[0]], small[1])
    inner = own.shape[1]
    indices = Indices(small[0], inner - 1, 8 - inner)
    me = lax.axis_index("gy")
    slots = packed.shape[1]
    near_pick[...] = jnp.zeros_like(near_pick)
    far_pick[...] = jnp.zeros_like(far_pick)
    near_lane = lax.broadcasted_iota(I32, (1, near_pick.shape[1]), 1)
    far_lane = lax.broadcasted_iota(I32, (1, far_pick.shape[1]), 1)
    count = got0.shape[1] // BLK
    blocks = density.shape[0]
    tables = tables_of(got0, count) + tables_of(got1, count)
    last = [wide(table[6:7, :]) for table in tables]
    for b in range(blocks):
        density[b : b + 1, :] = state[6:7, chunk(b)]
    for v in range(blocks // 8):
        part = slice(8 * v, 8 * v + 8)
        density[part, :] = patch(density[part, :], codes[0, part, :], last)

    for copy in copies:
        copy.wait()
    for n in range(TOTACT):
        wanted = [indices.active(n)] + indices.near_blocks(n)
        for t, block in enumerate(wanted):
            own[n, t] = early_block(state, codes, tables, block)
            near_pick[8 * n + t : 8 * n + t + 1, :] = jnp.where(near_lane == block, 1.0, 0.0)
        for t, g in enumerate(indices.ghosts(n, me * slots)):
            at = 8 * n + inner + t
            far_pick[at : at + 1, :] = jnp.where(far_lane == g, 1.0, 0.0)


def spread(rows, out, kept):
    columns_of = jnp.transpose(jnp.concatenate((rows + rows)[:8], axis=0))
    for k in range(len(rows)):
        values = jnp.broadcast_to(columns_of[:, k : k + 1], (BLK, BLK))
        out[k] = values
        if k < 5:
            kept[k] = values


def added(old, value):
    return value if old is None else old + value


def pair_weight(distance, h1, h2, m1, m2):
    inverse = 1.0 / (h1 + h2)
    inv2 = inverse * inverse
    slope = jnp.maximum(inverse - distance * inv2, 0.0)
    return slope * slope * slope * inv2 * (m1 * m2)


def pair_sums(near, n, centre, inside, outside, press, fresh, others):
    local = inside.shape[1] // BLK
    far = 8 - local
    row = lax.broadcasted_iota(I32, (8, BLK), 0)
    lane = lax.broadcasted_iota(I32, (8, BLK), 1)
    plain = [[None] * 3 for _ in range(far)]
    pressed = [[None] * 3 for _ in range(far)]
    own = None
    waiting = None

    def settle_pushes(pushes, pressure):
        for t in range(far):
            for k in range(3):
                pressed[t][k] = added(pressed[t][k], pushes[t][k] * pressure)

    for g in range(BLK // 8):
        part = slice(8 * g, 8 * g + 8)
        cx, cy, cz, cm, ch, cu = (centre[k, part, :] for k in range(6))
        half = 0.5 / ch
        total = None
        pushes = []
        for t in range(8):
            x, y, z, m, h = (wide(near[n, k, t : t + 1, :]) for k in range(5))
            apart = (cx - x, cy - y, cz - z)
            square = apart[0] * apart[0] + apart[1] * apart[1] + apart[2] * apart[2]
            distance = square * lax.rsqrt(jnp.maximum(square, TINY))
            fall = jnp.maximum(1.0 - distance * half, 0.0)
            fall2 = fall * fall
            total = added(total, fall2 * fall2 * (1.25 - fall) * m)
            if t < local:
                at = 8 * (g * local + t)
                inside[n, at : at + 8, :] = distance
            else:
                weight = pair_weight(distance, ch, h, cm, m)
                at = 8 * (g * far + t - local)
                push = [weight * apart[k] for k in range(3)]
                for k in range(3):
                    outside[n, k, at : at + 8, :] = push[k]
                    plain[t - local][k] = added(plain[t - local][k], push[k])
                pushes.append(push)
        total = jnp.broadcast_to(jnp.sum(total, axis=1, keepdims=True), (8, BLK))
        rho = total * (4.0 * KERNEL_NORM / (ch * ch * ch))
        pressure = cu / rho
        press[n, part, :] = pressure
        own = added(own, jnp.where(row + 8 * g == lane, rho, 0.0))
        if waiting is not None:
            settle_pushes(*waiting)
        waiting = (pushes, pressure)
    settle_pushes(*waiting)
    fresh[pl.ds(n, 1), :] = jnp.sum(own, axis=0, keepdims=True)
    for t in range(far):
        for k in range(3):
            at = 8 * (k * far + t)
            others[n, at : at + 8, :] = pressed[t][k]
            at = 8 * ((3 + k) * far + t)
            others[n, at : at + 8, :] = plain[t][k]


def make_density_kernel(peers, slots):
    def density_kernel(own, before, codes, packed, *refs):
        sent = by_partner(refs[:peers], BLOCK_ORDER)
        near, density, centre, press, inside, outside = refs[peers : peers + 6]
        outs = refs[peers + 6 : 2 * peers + 6]
        (late_three, ghosts, first, second, fresh, others, rows, back, *small) = refs[
            2 * peers + 6 :
        ]
        copies = fetch([packed], [small[0]], small[1])
        inner = own.shape[1]
        ngh = 8 - inner
        indices = Indices(small[0], inner - 1, ngh)
        count = late_three.shape[2] // BLK
        blocks = density.shape[0]
        row = lax.broadcasted_iota(I32, (8, BLK), 0)
        me = lax.axis_index("gy")

        for q in range(peers):
            items, code_row = unpacked(sent[q], 2 * count + slots)
            tables = tables_of(sent[q ^ 2], count)
            for c in range(count):
                values = items[count + c]
                code = wide(values[code_row : code_row + 1, :]).astype(I32)
                if q == 1:
                    values = jnp.where(row == 6, wide(items[c][6:7, :]), values)
                late_three[q, :, chunk(c)] = patch(values, code, tables)

        def settle(values, q, code_row=7):
            code = wide(values[code_row : code_row + 1, :]).astype(I32)
            tables = tables_of(sent[q ^ 2], count)
            tables += [late_three[q ^ 1, :, chunk(c)] for c in range(count)]
            return patch(values, code, tables)

        for q in range(peers):
            items, code_row = unpacked(sent[q], 2 * count + slots)
            for t in range(slots):
                ghosts[:, chunk(q * slots + t)] = settle(items[2 * count + t], q, code_row)

        later = [sent[2][6:7, chunk(c)] for c in range(count)]
        later = [wide(x) for x in later + [late_three[1, 6:7, chunk(c)] for c in range(count)]]
        for v in range(blocks // 8):
            part = slice(8 * v, 8 * v + 8)
            density[part, :] = patch(before[part, :], codes[1, part, :], later)
        back[...] = jnp.zeros_like(back)

        for copy in copies:
            copy.wait()
        live = indices.live()

        for n in range(TOTACT):
            for t in range(inner):
                near[n, :, t, :] = settle(own[n, t], 0)
            for t, g in enumerate(indices.ghosts(n, me * slots)):
                near[n, :, inner + t, :] = ghosts[:, lanes(g)]

        def prepare(n, buffer):
            spread([near[n, k, 0:1, :] for k in range(6)], buffer, centre.at[n])

        def work(n, buffer):
            pair_sums(near, n, buffer, inside, outside, press, fresh, others)

        prepare(0, first)

        def step(p, _):
            n = 2 * p
            prepare(n + 1, second)
            work(n, first)
            prepare(jnp.minimum(n + 2, TOTACT - 1), first)
            work(n + 1, second)
            return 0

        lax.fori_loop(0, (live + 1) // 2, step, 0)
        for n in range(TOTACT):
            for t in range(ngh):
                m = near[n, 3, inner + t : inner + t + 1, :]
                u = near[n, 5, inner + t : inner + t + 1, :]
                scale = -FORCE_NORM / m
                for k in range(6):
                    row = 8 * (k * ngh + t)
                    total = jnp.sum(others[n, row : row + 8, :], axis=0, keepdims=True)
                    rows[n, k, t : t + 1, :] = total * (scale if k < 3 else scale * u)

        for n in range(TOTACT):
            for t, g in enumerate(indices.ghosts(n, me * slots)):
                back[0:6, lanes(g)] += jnp.where(n < live, rows[n, 0:6, t, :], 0.0)

        def place(n, _):
            density[pl.ds(indices.active(n), 1), :] = fresh[pl.ds(n, 1), :]
            return 0

        lax.fori_loop(0, live, place, 0)
        for q in range(peers):
            outs[q][...] = back[:, q * slots * BLK : (q + 1) * slots * BLK]
            for t in range(slots):
                rho = density[pl.ds(indices.exported(me ^ q, t), 1), :]
                outs[q][6:7, chunk(t)] = rho

    return density_kernel


def inner_sums(near, n, centre, press, others_press, inside, sums, others):
    local = inside.shape[1] // BLK
    pushed = [[None] * 3 for _ in range(local)]
    for g in range(BLK // 8):
        part = slice(8 * g, 8 * g + 8)
        *here, cm, ch = (centre[n, k, part, :] for k in range(5))
        cp = press[n, part, :]
        total = [None] * 3
        for t in range(local):
            *tile, m, h = (wide(near[n, k, t : t + 1, :]) for k in range(5))
            row = 8 * (g * local + t)
            weight = pair_weight(inside[n, row : row + 8, :], ch, h, cm, m)
            weight = weight * (cp + wide(others_press[n, t : t + 1, :]))
            for k in range(3):
                push = weight * (here[k] - tile[k])
                total[k] = push if total[k] is None else total[k] + push
                if t > 0:
                    old = pushed[t][k]
                    pushed[t][k] = push if old is None else old + push
        for k in range(3):
            sums[n, k, part, :] = total[k]
    for t in range(1, local):
        for k in range(3):
            row = 8 * (k * local + t)
            others[n, row : row + 8, :] = pushed[t][k]


def inner_kernel(
    near, density, centre, press, inside, near_pick, packed, totals, sums, *refs
):
    others_press, others, rows, *small = refs
    copies = fetch([packed], [small[0]], small[1])
    inner = inside.shape[1] // BLK
    indices = Indices(small[0], inner - 1, 8 - inner)
    totals[...] = jnp.zeros_like(totals)
    rho = picked_rows(near_pick[...], density[...])
    for n in range(TOTACT):
        others_press[n] = near[n, 5] / rho[8 * n : 8 * n + 8]

    def step(n, _):
        inner_sums(near, n, centre, press, others_press, inside, sums, others)
        return 0

    lax.fori_loop(0, TOTACT, step, 0)
    for copy in copies:
        copy.wait()
    live = indices.live()
    for n in range(TOTACT):
        blocks = indices.near_blocks(n)
        for t in range(1, inner):
            scale = -FORCE_NORM / near[n, 3, t : t + 1, :]
            for k in range(3):
                row = 8 * (k * inner + t)
                total = jnp.sum(others[n, row : row + 8, :], axis=0, keepdims=True)
                rows[n, k, t : t + 1, :] = total * scale
            totals[0:3, lanes(blocks[t - 1])] += jnp.where(n < live, rows[n, 0:3, t, :], 0.0)


def outer_sums(near, n, press, others_press, outside, before, rows):
    far = outside.shape[2] // BLK
    theirs = [wide(others_press[n, t : t + 1, :]) for t in range(8 - far, 8)]
    row = lax.broadcasted_iota(I32, (8, BLK), 0)
    lane = lax.broadcasted_iota(I32, (8, BLK), 1)
    own = [None] * 3
    for g in range(BLK // 8):
        part = slice(8 * g, 8 * g + 8)
        cp = press[n, part, :]
        total = [before[n, k, part, :] for k in range(3)]
        for t in range(far):
            at = 8 * (g * far + t)
            both = cp + theirs[t]
            for k in range(3):
                total[k] = total[k] + both * outside[n, k, at : at + 8, :]
        for k in range(3):
            value = jnp.broadcast_to(jnp.sum(total[k], axis=1, keepdims=True), (8, BLK))
            own[k] = added(own[k], jnp.where(row + 8 * g == lane, value, 0.0))
    scale = FORCE_NORM / near[n, 3, 0:1, :]
    for k in range(3):
        rows[n, k : k + 1, :] = jnp.sum(own[k], axis=0, keepdims=True) * scale


def make_outer_kernel(peers, slots):
    def outer_kernel(
        near, density, press, outside, totals, before, far_pick, packed, *refs
    ):
        sent = refs[:peers]
        got = by_partner(refs[peers : 2 * peers], RETURN_ORDER)
        accel, density_out, out, far_rho, others_press, rows, sems, *small = refs[2 * peers :]
        density_copy = pltpu.make_async_copy(density, density_out, sems.at[PIECES])
        density_copy.start()
        copies = fetch([packed], [small[0]], small[1])
        ngh = outside.shape[2] // BLK
        indices = Indices(small[0], 7 - ngh, ngh)
        far_rho[...] = jnp.zeros_like(far_rho)
        for q in range(peers):
            for t in range(slots):
                g = q * slots + t
                far_rho[g : g + 1, :] = got[q][6:7, chunk(t)]
        out[...] = totals[0:3, :]
        rho = picked_rows(far_pick[...], far_rho[...])
        for n in range(TOTACT):
            others_press[n] = near[n, 5] / rho[8 * n : 8 * n + 8]

        def step(n, _):
            outer_sums(near, 2 * n, press, others_press, outside, before, rows)
            outer_sums(near, 2 * n + 1, press, others_press, outside, before, rows)
            return 0

        lax.fori_loop(0, TOTACT // 2, step, 0)
        for copy in copies:
            copy.wait()
        me = lax.axis_index("gy")
        live = indices.live()
        for q in range(peers):
            for t in range(slots):
                own_rho = sent[q][6:7, chunk(t)]
                value = got[q][0:3, chunk(t)] + got[q][3:6, chunk(t)] / own_rho
                out[0:3, lanes(indices.exported(me ^ q, t))] += value
        for n in range(TOTACT):
            out[0:3, lanes(indices.active(n))] += jnp.where(n < live, rows[n, 0:3, :], 0.0)
        size = out.shape[1] // PIECES
        copies = [density_copy]
        for p in range(PIECES):
            part = slice(p * size, (p + 1) * size)
            copy = pltpu.make_async_copy(out.at[:, part], accel.at[:, part], sems.at[p])
            copy.start()
            copies.append(copy)
        for copy in copies:
            copy.wait()

    return outer_kernel


def crossed(block, axis, bits):
    size = lax.axis_size(axis)
    return lax.ppermute(block, axis, [(i, i ^ bits) for i in range(size) if i ^ bits < size])


def first_steps(peers, first):
    return list(first) + [q for q in range(peers - 1, 0, -1) if q not in first]


def exchanged(parts, first):
    return [parts[0]] + [crossed(parts[q], "gy", q) for q in first_steps(len(parts), first)]


def by_partner(refs, first):
    steps = [0] + first_steps(len(refs), first)
    return [refs[steps.index(q)] for q in range(len(refs))]


def shards(
    particles, mig_count, mig_rows, active_ids, active_count, local_nbrs, ghost_slots, export_blocks
):
    peers = lax.axis_size("gy")
    slots = export_blocks.shape[2]
    per_dev = particles.shape[1]
    blocks = per_dev // BLK
    mig = mig_rows.shape[2]
    inner = 1 + local_nbrs.shape[3]
    wide_total = peers * slots * BLK

    ints = jnp.concatenate(
        [
            mig_rows[0],
            jnp.pad(mig_count, ((0, 3), (0, mig - 4))),
            jnp.pad(export_blocks[0], ((0, 0), (0, mig - slots))),
        ],
        axis=0,
    )
    state = jnp.pad(particles, ((0, 1), (0, 0)))
    sent0 = call(first_kernel, shape(8, mig), state, ints)
    codes = call(codes_kernel, shape(4, blocks, BLK, dtype=I32), ints)
    got0 = crossed(sent0, "gx", 2)
    cols1, marks1, tables = call(
        early_tables_kernel,
        [shape(8, mig), shape(8, mig, dtype=I32), shape(4, blocks, BLK, dtype=I32)],
        state,
        ints,
        codes,
    )
    sent1 = call(second_kernel, shape(8, mig), cols1, marks1, got0)
    got1 = crossed(sent1, "gx", 1)
    cols, raw, code_rows = call(
        late_tables_kernel,
        [
            shape(2, 8, mig),
            shape(8, wide_total),
            shape(peers, slots, BLK, dtype=I32),
        ],
        state,
        ints,
        tables,
        sent1,
        scratch=[SMEM((peers, BLK), I32), DMA((1,))],
    )
    packs = call(
        export_kernel,
        [
            shape(8, 2 * mig + slots * BLK if q == 0 else packed_width(mig, slots) * BLK)
            for q in range(peers)
        ],
        cols,
        marks1,
        got0,
        got1,
        raw,
        code_rows,
    )
    sent = exchanged(packs, BLOCK_ORDER)
    packed = shape(3 + 2 * 7 + peers, active_ids.shape[2], dtype=I32)
    own, before, near_pick, far_pick, packed = call(
        own_kernel,
        [
            shape(TOTACT, inner, 8, BLK),
            shape(blocks, BLK),
            shape(TOTACT * 8, blocks),
            shape(TOTACT * 8, max(BLK, peers * slots)),
            packed,
        ],
        state,
        got0,
        got1,
        tables,
        active_ids,
        active_count,
        jnp.transpose(local_nbrs, (0, 3, 1, 2)),
        jnp.transpose(ghost_slots, (0, 1, 3, 2)),
        export_blocks,
        scratch=fetch_scratch([packed]),
    )
    local = shape(TOTACT, inner * BLK, BLK)
    remote = shape(TOTACT, 3, (8 - inner) * BLK, BLK)
    near, density, centre, press, inside, outside, *returns = call(
        make_density_kernel(peers, slots),
        [
            shape(TOTACT, 8, 8, BLK),
            shape(blocks, BLK),
            shape(TOTACT, 5, BLK, BLK),
            shape(TOTACT, BLK, BLK),
            local,
            remote,
        ]
        + [shape(8, slots * BLK)] * peers,
        own,
        before,
        tables,
        packed,
        *sent,
        scratch=[
            VMEM((peers, 8, mig), F32),
            VMEM((8, wide_total), F32),
            VMEM((6, BLK, BLK), F32),
            VMEM((6, BLK, BLK), F32),
            VMEM((TOTACT, BLK), F32),
            VMEM((TOTACT, 6 * (8 - inner) * 8, BLK), F32),
            VMEM((TOTACT, 8, 8, BLK), F32),
            VMEM((8, wide_total), F32),
        ]
        + fetch_scratch([packed]),
    )
    got = exchanged(returns, RETURN_ORDER)
    totals, sums = call(
        inner_kernel,
        [shape(8, per_dev), shape(TOTACT, 3, BLK, BLK)],
        near,
        density,
        centre,
        press,
        inside,
        near_pick,
        packed,
        scratch=[
            VMEM((TOTACT, 8, BLK), F32),
            VMEM((TOTACT, 3 * inner * 8, BLK), F32),
            VMEM((TOTACT, 8, 8, BLK), F32),
        ]
        + fetch_scratch([packed]),
    )
    accel, density_out = call(
        make_outer_kernel(peers, slots),
        [shape(3, per_dev), shape(blocks, BLK)],
        near,
        density,
        press,
        outside,
        totals,
        sums,
        far_pick,
        packed,
        *returns,
        *got,
        out_any=True,
        scratch=[
            VMEM((3, per_dev), F32),
            VMEM((max(BLK, peers * slots), BLK), F32),
            VMEM((TOTACT, 8, BLK), F32),
            VMEM((TOTACT, 8, BLK), F32),
            DMA((PIECES + 1,)),
        ]
        + fetch_scratch([packed]),
    )
    return density_out.reshape(-1), accel


def solution(mesh):
    both = ("gx", "gy")
    placed = (
        P(None, both),
        P(both, None),
        P(both, None, None),
        P(both, None, None),
        P(both, None),
        P(both, None, None, None),
        P(both, None, None, None),
        P(both, None, None),
    )
    return jax.shard_map(
        shards,
        mesh=mesh,
        in_specs=placed,
        out_specs=(P(both), P(None, both)),
        check_vma=False,
    )
```

```python
import math

import jax
import jax.numpy as jnp
from jax import lax
from jax.experimental import pallas as pl
from jax.experimental.pallas import tpu as pltpu
from jax.sharding import PartitionSpec as P

BLK = 128
TOTACT = 12
KERNEL_NORM = 21.0 / (16.0 * math.pi)
FORCE_NORM = 5.0 * KERNEL_NORM * 32.0 * (2.0 / 3.0)
TINY = 1e-30
BLOCK_ORDER = (3, 2, 1)
RETURN_ORDER = (2, 3, 1)
PIECES = 8
F32 = jnp.float32
I32 = jnp.int32
VMEM = pltpu.VMEM
SMEM = pltpu.SMEM
DMA = pltpu.SemaphoreType.DMA


def call(kernel, out_shape, *args, smem=(), scratch=(), limit=16 << 20, out_any=False):
    def space(n):
        return SMEM if n in smem else VMEM

    return pl.pallas_call(
        kernel,
        out_shape=out_shape,
        in_specs=[pl.BlockSpec(memory_space=space(n)) for n in range(len(args))],
        out_specs=jax.tree.map(
            lambda _: pl.BlockSpec(memory_space=pl.ANY if out_any else VMEM), out_shape
        ),
        scratch_shapes=list(scratch),
        compiler_params=pltpu.CompilerParams(vmem_limit_bytes=limit),
    )(*args)


def shape(*dims, dtype=F32):
    return jax.ShapeDtypeStruct(dims, dtype)


def wide(row):
    return jnp.broadcast_to(row, (8, BLK))


def lanes(block):
    return pl.ds(pl.multiple_of(block * BLK, BLK), BLK)


def chunk(c):
    return slice(c * BLK, (c + 1) * BLK)


def take(values, index):
    return jnp.take_along_axis(values, index, axis=1)


def patch(values, code, tables):
    lane = code & (BLK - 1)
    which = code >> 7
    for n, table in enumerate(tables):
        values = jnp.where(which == n, take(table, lane), values)
    return values


def tables_of(ref, count, start=0):
    return [ref[:, chunk(start + c)] for c in range(count)]


def columns(state, slots):
    block = slots >> 7
    lane = slots & (BLK - 1)
    found = jnp.zeros((8, BLK), F32)
    for b in range(state.shape[1] // BLK):
        found = jnp.where(block == b, take(state[:, chunk(b)], lane), found)
    return found


def fetch(sources, targets, sems):
    copies = [
        pltpu.make_async_copy(a, b, sems.at[n]) for n, (a, b) in enumerate(zip(sources, targets))
    ]
    for copy in copies:
        copy.start()
    return copies


def fetch_scratch(arrays):
    return [SMEM(a.shape, I32) for a in arrays] + [DMA((len(arrays),))]


def first_kernel(state, ints, out):
    for c in range(ints.shape[1] // BLK):
        out[:, chunk(c)] = columns(state, wide(ints[0:1, chunk(c)]))


def code_table(ints, level, blocks):
    mig = ints.shape[1]
    slots = ints[level : level + 1, :]
    k = lax.broadcasted_iota(I32, (1, mig), 1)
    low = (k & (BLK - 1)).astype(F32)
    high = ((k >> 7) + 1).astype(F32)
    in_block = lax.broadcasted_iota(I32, (blocks, mig), 0) == (slots >> 7)
    in_lane = lax.broadcasted_iota(I32, (BLK, mig), 0) == (slots & (BLK - 1))
    left = jnp.concatenate([jnp.where(in_block, low, 0.0), jnp.where(in_block, high, 0.0)], axis=0)
    right = jnp.where(in_lane, 1.0, 0.0)
    both = lax.dot_general(
        left.astype(jnp.bfloat16),
        right.astype(jnp.bfloat16),
        (((1,), (1,)), ((), ())),
        preferred_element_type=F32,
    )
    low, high = both[:blocks], both[blocks:]
    return jnp.where(high > 0.5, (high - 1.0) * BLK + low, -1.0).astype(I32)


def codes_kernel(ints, codes):
    for level in range(4):
        codes[level] = code_table(ints, level, codes.shape[1])


def code_at(table, slots):
    block = slots >> 7
    lane = slots & (BLK - 1)
    row = lax.broadcasted_iota(I32, (8, BLK), 0)
    found = jnp.full((8, BLK), -1, I32)
    for v in range(table.shape[0] // 8):
        piece = take(table[8 * v : 8 * v + 8, :], lane)
        found = jnp.where(block == row + 8 * v, piece, found)
    return jnp.max(found, axis=0, keepdims=True)


def early_tables_kernel(state, ints, codes, cols, marks, tables):
    mig = ints.shape[1]
    valid = []
    for level in range(4):
        code = codes[level]
        valid.append(jnp.where(code < ints[4:5, level : level + 1], code, -1))
    tables[0] = jnp.where(valid[1] >= 0, valid[1] + mig, valid[0])
    tables[1] = jnp.where(valid[3] >= 0, valid[3] + mig, valid[2])
    tables[2] = valid[2]
    tables[3] = valid[0]
    for c in range(mig // BLK):
        slots = wide(ints[1:2, chunk(c)])
        two, three = (wide(ints[level : level + 1, chunk(c)]) for level in (2, 3))
        marks[0:1, chunk(c)] = code_at(tables.at[3], slots)
        marks[1:2, chunk(c)] = code_at(tables.at[0], two)
        marks[2:3, chunk(c)] = code_at(tables.at[0], three)
        marks[3:4, chunk(c)] = code_at(tables.at[2], three)
        cols[:, chunk(c)] = columns(state, slots)


def late_tables_kernel(
    state, ints, tables, after, cols, raw, code_rows, exported, sems
):
    peers, slots, _ = code_rows.shape
    copies = fetch([ints.at[pl.ds(8, peers), pl.ds(0, BLK)]], [exported], sems)
    for c in range(ints.shape[1] // BLK):
        two, three = (wide(ints[level : level + 1, chunk(c)]) for level in (2, 3))
        cols[0, :, chunk(c)] = columns(state, two)
        cols[1, :, chunk(c)] = columns(state, three)
    for copy in copies:
        copy.wait()
    me = lax.axis_index("gy")
    row = lax.broadcasted_iota(I32, (8, BLK), 0)
    for q in range(peers):
        for t in range(slots):
            block = exported[me ^ q, t]
            code = wide(tables[1, pl.ds(block, 1), :]).astype(F32)
            raw[:, chunk(q * slots + t)] = jnp.where(row == 7, code, state[:, lanes(block)])
            code_rows[q, t : t + 1, :] = tables[0, pl.ds(block, 1), :]


def second_kernel(cols, marks, got0, out):
    count = got0.shape[1] // BLK
    tables = tables_of(got0, count)
    for c in range(count):
        out[:, chunk(c)] = patch(cols[:, chunk(c)], wide(marks[0:1, chunk(c)]), tables)


def early_block(state, codes, tables, block):
    row = lax.broadcasted_iota(I32, (8, BLK), 0)
    patched = patch(state[:, lanes(block)], wide(codes[0, pl.ds(block, 1), :]), tables)
    return jnp.where(row == 7, wide(codes[1, pl.ds(block, 1), :]).astype(F32), patched)


def packed_width(mig, slots):
    total = mig * 2 // BLK + slots
    return total - total // 8


def export_kernel(cols, marks, got0, got1, raw, code_rows, *outs):
    count = got0.shape[1] // BLK
    slots = code_rows.shape[1]
    tables = tables_of(got0, count) + tables_of(got1, count)
    row = lax.broadcasted_iota(I32, (8, BLK), 0)
    twos, threes = [], []
    for c in range(count):
        twos.append(patch(cols[0, :, chunk(c)], wide(marks[1:2, chunk(c)]), tables))
        three = patch(cols[1, :, chunk(c)], wide(marks[2:3, chunk(c)]), tables)
        threes.append((three, wide(marks[3:4, chunk(c)]).astype(F32)))
    for q, out in enumerate(outs):
        coded = list(threes)
        for t in range(slots):
            values = raw[:, chunk(q * slots + t)]
            patched = patch(values, wide(code_rows[q, t : t + 1, :]), tables)
            coded.append((patched, wide(values[7:8, :])))
        code_row = 7 if q == 0 else 6
        items = list(twos)
        if q == 1:
            for c in range(count):
                items[c] = jnp.where(row == 6, wide(threes[c][0][6:7, :]), twos[c])
        items += [jnp.where(row == code_row, code, v) for v, code in coded]
        kept = out.shape[1] // BLK
        for i in range(kept):
            item = items[i]
            if kept < len(items):
                item = jnp.where(row == 7, wide(items[kept + i // 7][i % 7 : i % 7 + 1, :]), item)
            out[:, chunk(i)] = item


def unpacked(ref, total):
    kept = ref.shape[1] // BLK
    items = [ref[:, chunk(i)] for i in range(kept)]
    for extra in range(total - kept):
        rows = [ref[7:8, chunk(7 * extra + r)] for r in range(7)]
        items.append(jnp.concatenate(rows + rows[:1], axis=0))
    return items, 7 if kept == total else 6


class Indices:
    def __init__(self, ref, near, far):
        self.ref, self.near, self.far = ref, near, far
        self.counts = 2 + 2 * (near + far)

    def live(self):
        return self.ref[self.counts, 0] + self.ref[self.counts, 1]

    def slot(self, n):
        first = self.ref[self.counts, 0]
        second = n >= first
        last = self.ref.shape[1] - 1
        return jnp.where(second, 1, 0), jnp.where(second, jnp.minimum(n - first, last), n)

    def active(self, n):
        which, i = self.slot(n)
        return self.ref[which, i]

    def near_blocks(self, n):
        which, i = self.slot(n)
        return [self.ref[2 + 2 * t + which, i] for t in range(self.near)]

    def ghosts(self, n, mine):
        which, i = self.slot(n)
        start = 2 + 2 * self.near + which * self.far
        return [self.ref[start + t, i] ^ mine for t in range(self.far)]

    def exported(self, place, t):
        return self.ref[self.counts + 1 + place, t]


def pack_indices(packed, ids, counts, nbrs, far, exports):
    packed[...] = jnp.zeros_like(packed)
    packed[0:2, :] = ids[0]
    at = 2
    for part in (nbrs, far):
        for k in range(part.shape[1]):
            packed[at : at + part.shape[2], :] = part[0, k]
            at += part.shape[2]
    packed[at : at + 1, 0:2] = counts[...]
    packed[at + 1 : at + 1 + exports.shape[1], :] = exports[0]


def picked_rows(chosen, table):
    high = table.astype(jnp.bfloat16)
    rest = table - high.astype(F32)
    middle = rest.astype(jnp.bfloat16)
    low = (rest - middle.astype(F32)).astype(jnp.bfloat16)
    chosen = chosen.astype(jnp.bfloat16)
    return jnp.dot(
        jnp.concatenate([chosen] * 3, axis=1),
        jnp.concatenate([high, middle, low], axis=0),
        preferred_element_type=F32,
    )


def own_kernel(
    state, got0, got1, codes, ids, counts, nbrs, far, exports, own, density, near_pick, far_pick,
    packed, *small
):
    pack_indices(packed, ids, counts, nbrs, far, exports)
    copies = fetch([packed], [small[0]], small[1])
    inner = own.shape[1]
    indices = Indices(small[0], inner - 1, 8 - inner)
    me = lax.axis_index("gy")
    slots = packed.shape[1]
    near_pick[...] = jnp.zeros_like(near_pick)
    far_pick[...] = jnp.zeros_like(far_pick)
    near_lane = lax.broadcasted_iota(I32, (1, near_pick.shape[1]), 1)
    far_lane = lax.broadcasted_iota(I32, (1, far_pick.shape[1]), 1)
    count = got0.shape[1] // BLK
    blocks = density.shape[0]
    tables = tables_of(got0, count) + tables_of(got1, count)
    last = [wide(table[6:7, :]) for table in tables]
    for b in range(blocks):
        density[b : b + 1, :] = state[6:7, chunk(b)]
    for v in range(blocks // 8):
        part = slice(8 * v, 8 * v + 8)
        density[part, :] = patch(density[part, :], codes[0, part, :], last)

    for copy in copies:
        copy.wait()
    for n in range(TOTACT):
        wanted = [indices.active(n)] + indices.near_blocks(n)
        for t, block in enumerate(wanted):
            own[n, t] = early_block(state, codes, tables, block)
            near_pick[8 * n + t : 8 * n + t + 1, :] = jnp.where(near_lane == block, 1.0, 0.0)
        for t, g in enumerate(indices.ghosts(n, me * slots)):
            at = 8 * n + inner + t
            far_pick[at : at + 1, :] = jnp.where(far_lane == g, 1.0, 0.0)


def spread(rows, out, kept):
    columns_of = jnp.transpose(jnp.concatenate((rows + rows)[:8], axis=0))
    for k in range(len(rows)):
        values = jnp.broadcast_to(columns_of[:, k : k + 1], (BLK, BLK))
        out[k] = values
        if k < 5:
            kept[k] = values


def added(old, value):
    return value if old is None else old + value


def pair_weight(distance, h1, h2, m1, m2):
    inverse = 1.0 / (h1 + h2)
    inv2 = inverse * inverse
    slope = jnp.maximum(inverse - distance * inv2, 0.0)
    return slope * slope * slope * inv2 * (m1 * m2)


def pair_sums(near, n, centre, inside, outside, press, fresh, others):
    local = inside.shape[1] // BLK
    far = 8 - local
    row = lax.broadcasted_iota(I32, (8, BLK), 0)
    lane = lax.broadcasted_iota(I32, (8, BLK), 1)
    plain = [[None] * 3 for _ in range(far)]
    pressed = [[None] * 3 for _ in range(far)]
    own = None
    waiting = None

    def settle_pushes(pushes, pressure):
        for t in range(far):
            for k in range(3):
                pressed[t][k] = added(pressed[t][k], pushes[t][k] * pressure)

    for g in range(BLK // 8):
        part = slice(8 * g, 8 * g + 8)
        cx, cy, cz, cm, ch, cu = (centre[k, part, :] for k in range(6))
        reach = 2.0 * ch
        edge = 2.5 * ch
        total = None
        pushes = []
        for t in (4, 0, 5, 1, 6, 2, 7, 3):
            x, y, z, m, h = (wide(near[n, k, t : t + 1, :]) for k in range(5))
            apart = (cx - x, cy - y, cz - z)
            square = apart[0] * apart[0] + apart[1] * apart[1] + apart[2] * apart[2]
            distance = square * lax.rsqrt(jnp.maximum(square, TINY))
            fall = jnp.maximum(reach - distance, 0.0)
            fall2 = fall * fall
            total = added(total, fall2 * fall2 * (edge - fall) * m)
            if t < local:
                at = 8 * (g * local + t)
                inside[n, at : at + 8, :] = distance
            else:
                weight = pair_weight(distance, ch, h, cm, m)
                at = 8 * (g * far + t - local)
                push = [weight * apart[k] for k in range(3)]
                for k in range(3):
                    outside[n, k, at : at + 8, :] = push[k]
                    plain[t - local][k] = added(plain[t - local][k], push[k])
                pushes.append(push)
        total = jnp.broadcast_to(jnp.sum(total, axis=1, keepdims=True), (8, BLK))
        inverse = 1.0 / reach
        inv2 = inverse * inverse
        rho = total * (inv2 * inv2 * inverse) * ((32.0 * KERNEL_NORM) * (inv2 * inverse))
        pressure = cu / rho
        press[n, part, :] = pressure
        own = added(own, jnp.where(row + 8 * g == lane, rho, 0.0))
        if waiting is not None:
            settle_pushes(*waiting)
        waiting = (pushes, pressure)
    settle_pushes(*waiting)
    fresh[pl.ds(n, 1), :] = jnp.sum(own, axis=0, keepdims=True)
    for t in range(far):
        for k in range(3):
            at = 8 * (k * far + t)
            others[n, at : at + 8, :] = pressed[t][k]
            at = 8 * ((3 + k) * far + t)
            others[n, at : at + 8, :] = plain[t][k]


def make_density_kernel(peers, slots):
    def density_kernel(own, before, codes, packed, *refs):
        sent = by_partner(refs[:peers], BLOCK_ORDER)
        near, density, centre, press, inside, outside = refs[peers : peers + 6]
        outs = refs[peers + 6 : 2 * peers + 6]
        (late_three, ghosts, first, second, fresh, others, rows, back, *small) = refs[
            2 * peers + 6 :
        ]
        copies = fetch([packed], [small[0]], small[1])
        inner = own.shape[1]
        ngh = 8 - inner
        indices = Indices(small[0], inner - 1, ngh)
        count = late_three.shape[2] // BLK
        blocks = density.shape[0]
        row = lax.broadcasted_iota(I32, (8, BLK), 0)
        me = lax.axis_index("gy")

        for q in range(peers):
            items, code_row = unpacked(sent[q], 2 * count + slots)
            tables = tables_of(sent[q ^ 2], count)
            for c in range(count):
                values = items[count + c]
                code = wide(values[code_row : code_row + 1, :]).astype(I32)
                if q == 1:
                    values = jnp.where(row == 6, wide(items[c][6:7, :]), values)
                late_three[q, :, chunk(c)] = patch(values, code, tables)

        def settle(values, q, code_row=7):
            code = wide(values[code_row : code_row + 1, :]).astype(I32)
            tables = tables_of(sent[q ^ 2], count)
            tables += [late_three[q ^ 1, :, chunk(c)] for c in range(count)]
            return patch(values, code, tables)

        for q in range(peers):
            items, code_row = unpacked(sent[q], 2 * count + slots)
            for t in range(slots):
                ghosts[:, chunk(q * slots + t)] = settle(items[2 * count + t], q, code_row)

        later = [sent[2][6:7, chunk(c)] for c in range(count)]
        later = [wide(x) for x in later + [late_three[1, 6:7, chunk(c)] for c in range(count)]]
        for v in range(blocks // 8):
            part = slice(8 * v, 8 * v + 8)
            density[part, :] = patch(before[part, :], codes[1, part, :], later)
        back[...] = jnp.zeros_like(back)

        for copy in copies:
            copy.wait()
        live = indices.live()

        for n in range(TOTACT):
            for t in range(inner):
                near[n, :, t, :] = settle(own[n, t], 0)
            for t, g in enumerate(indices.ghosts(n, me * slots)):
                near[n, :, inner + t, :] = ghosts[:, lanes(g)]

        def prepare(n, buffer):
            spread([near[n, k, 0:1, :] for k in range(6)], buffer, centre.at[n])

        def work(n, buffer):
            pair_sums(near, n, buffer, inside, outside, press, fresh, others)

        prepare(0, first)

        def step(p, _):
            n = 2 * p
            prepare(n + 1, second)
            work(n, first)
            prepare(jnp.minimum(n + 2, TOTACT - 1), first)
            work(n + 1, second)
            return 0

        lax.fori_loop(0, (live + 1) // 2, step, 0)
        for n in range(TOTACT):
            for t in range(ngh):
                m = near[n, 3, inner + t : inner + t + 1, :]
                u = near[n, 5, inner + t : inner + t + 1, :]
                scale = -FORCE_NORM / m
                for k in range(6):
                    row = 8 * (k * ngh + t)
                    total = jnp.sum(others[n, row : row + 8, :], axis=0, keepdims=True)
                    rows[n, k, t : t + 1, :] = total * (scale if k < 3 else scale * u)

        for n in range(TOTACT):
            for t, g in enumerate(indices.ghosts(n, me * slots)):
                back[0:6, lanes(g)] += jnp.where(n < live, rows[n, 0:6, t, :], 0.0)

        for n in range(TOTACT):
            block = pl.ds(indices.active(n), 1)
            density[block, :] = jnp.where(n < live, fresh[n : n + 1, :], density[block, :])
        for q in range(peers):
            outs[q][...] = back[:, q * slots * BLK : (q + 1) * slots * BLK]
            for t in range(slots):
                rho = density[pl.ds(indices.exported(me ^ q, t), 1), :]
                outs[q][6:7, chunk(t)] = rho

    return density_kernel


def inner_sums(near, n, centre, press, others_press, inside, sums, others):
    local = inside.shape[1] // BLK
    pushed = [[None] * 3 for _ in range(local)]
    for g in range(BLK // 8):
        part = slice(8 * g, 8 * g + 8)
        *here, cm, ch = (centre[n, k, part, :] for k in range(5))
        cp = press[n, part, :]
        total = [None] * 3
        for t in range(local):
            *tile, m, h = (wide(near[n, k, t : t + 1, :]) for k in range(5))
            row = 8 * (g * local + t)
            weight = pair_weight(inside[n, row : row + 8, :], ch, h, cm, m)
            weight = weight * (cp + wide(others_press[n, t : t + 1, :]))
            for k in range(3):
                push = weight * (here[k] - tile[k])
                total[k] = push if total[k] is None else total[k] + push
                if t > 0:
                    old = pushed[t][k]
                    pushed[t][k] = push if old is None else old + push
        for k in range(3):
            sums[n, k, part, :] = total[k]
    for t in range(1, local):
        for k in range(3):
            row = 8 * (k * local + t)
            others[n, row : row + 8, :] = pushed[t][k]


def inner_kernel(
    near, density, centre, press, inside, near_pick, packed, totals, sums, *refs
):
    others_press, others, rows, *small = refs
    copies = fetch([packed], [small[0]], small[1])
    inner = inside.shape[1] // BLK
    indices = Indices(small[0], inner - 1, 8 - inner)
    totals[...] = jnp.zeros_like(totals)
    rho = picked_rows(near_pick[...], density[...])
    for n in range(TOTACT):
        others_press[n] = near[n, 5] / rho[8 * n : 8 * n + 8]

    def step(n, _):
        inner_sums(near, n, centre, press, others_press, inside, sums, others)
        return 0

    lax.fori_loop(0, TOTACT, step, 0)
    for copy in copies:
        copy.wait()
    live = indices.live()
    for n in range(TOTACT):
        blocks = indices.near_blocks(n)
        for t in range(1, inner):
            scale = -FORCE_NORM / near[n, 3, t : t + 1, :]
            for k in range(3):
                row = 8 * (k * inner + t)
                total = jnp.sum(others[n, row : row + 8, :], axis=0, keepdims=True)
                rows[n, k, t : t + 1, :] = total * scale
            totals[0:3, lanes(blocks[t - 1])] += jnp.where(n < live, rows[n, 0:3, t, :], 0.0)


def outer_sums(near, n, press, others_press, outside, before, rows):
    far = outside.shape[2] // BLK
    theirs = [wide(others_press[n, t : t + 1, :]) for t in range(8 - far, 8)]
    row = lax.broadcasted_iota(I32, (8, BLK), 0)
    lane = lax.broadcasted_iota(I32, (8, BLK), 1)
    own = [None] * 3
    for g in range(BLK // 8):
        part = slice(8 * g, 8 * g + 8)
        cp = press[n, part, :]
        total = [before[n, k, part, :] for k in range(3)]
        for t in range(far):
            at = 8 * (g * far + t)
            both = cp + theirs[t]
            for k in range(3):
                total[k] = total[k] + both * outside[n, k, at : at + 8, :]
        for k in range(3):
            value = jnp.broadcast_to(jnp.sum(total[k], axis=1, keepdims=True), (8, BLK))
            own[k] = added(own[k], jnp.where(row + 8 * g == lane, value, 0.0))
    scale = FORCE_NORM / near[n, 3, 0:1, :]
    for k in range(3):
        rows[n, k : k + 1, :] = jnp.sum(own[k], axis=0, keepdims=True) * scale


def make_outer_kernel(peers, slots):
    def outer_kernel(
        near, density, press, outside, totals, before, far_pick, packed, *refs
    ):
        sent = refs[:peers]
        got = by_partner(refs[peers : 2 * peers], RETURN_ORDER)
        accel, density_out, out, far_rho, others_press, rows, sems, *small = refs[2 * peers :]
        density_copy = pltpu.make_async_copy(density, density_out, sems.at[PIECES])
        density_copy.start()
        copies = fetch([packed], [small[0]], small[1])
        ngh = outside.shape[2] // BLK
        indices = Indices(small[0], 7 - ngh, ngh)
        far_rho[...] = jnp.zeros_like(far_rho)
        for q in range(peers):
            for t in range(slots):
                g = q * slots + t
                far_rho[g : g + 1, :] = got[q][6:7, chunk(t)]
        out[...] = totals[0:3, :]
        rho = picked_rows(far_pick[...], far_rho[...])
        for n in range(TOTACT):
            others_press[n] = near[n, 5] / rho[8 * n : 8 * n + 8]

        def step(n, _):
            for k in range(4):
                outer_sums(near, 4 * n + k, press, others_press, outside, before, rows)
            return 0

        lax.fori_loop(0, TOTACT // 4, step, 0)
        for copy in copies:
            copy.wait()
        me = lax.axis_index("gy")
        live = indices.live()
        for q in range(peers):
            for t in range(slots):
                own_rho = sent[q][6:7, chunk(t)]
                value = got[q][0:3, chunk(t)] + got[q][3:6, chunk(t)] / own_rho
                out[0:3, lanes(indices.exported(me ^ q, t))] += value
        for n in range(TOTACT):
            out[0:3, lanes(indices.active(n))] += jnp.where(n < live, rows[n, 0:3, :], 0.0)
        size = out.shape[1] // PIECES
        copies = [density_copy]
        for p in range(PIECES):
            part = slice(p * size, (p + 1) * size)
            copy = pltpu.make_async_copy(out.at[:, part], accel.at[:, part], sems.at[p])
            copy.start()
            copies.append(copy)
        for copy in copies:
            copy.wait()

    return outer_kernel


def crossed(block, axis, bits):
    size = lax.axis_size(axis)
    return lax.ppermute(block, axis, [(i, i ^ bits) for i in range(size) if i ^ bits < size])


def first_steps(peers, first):
    return list(first) + [q for q in range(peers - 1, 0, -1) if q not in first]


def exchanged(parts, first):
    return [parts[0]] + [crossed(parts[q], "gy", q) for q in first_steps(len(parts), first)]


def by_partner(refs, first):
    steps = [0] + first_steps(len(refs), first)
    return [refs[steps.index(q)] for q in range(len(refs))]


def shards(
    particles, mig_count, mig_rows, active_ids, active_count, local_nbrs, ghost_slots, export_blocks
):
    peers = lax.axis_size("gy")
    slots = export_blocks.shape[2]
    per_dev = particles.shape[1]
    blocks = per_dev // BLK
    mig = mig_rows.shape[2]
    inner = 1 + local_nbrs.shape[3]
    wide_total = peers * slots * BLK

    ints = jnp.concatenate(
        [
            mig_rows[0],
            jnp.pad(mig_count, ((0, 3), (0, mig - 4))),
            jnp.pad(export_blocks[0], ((0, 0), (0, mig - slots))),
        ],
        axis=0,
    )
    state = jnp.pad(particles, ((0, 1), (0, 0)))
    sent0 = call(first_kernel, shape(8, mig), state, ints)
    codes = call(codes_kernel, shape(4, blocks, BLK, dtype=I32), ints)
    got0 = crossed(sent0, "gx", 2)
    cols1, marks1, tables = call(
        early_tables_kernel,
        [shape(8, mig), shape(8, mig, dtype=I32), shape(4, blocks, BLK, dtype=I32)],
        state,
        ints,
        codes,
    )
    sent1 = call(second_kernel, shape(8, mig), cols1, marks1, got0)
    got1 = crossed(sent1, "gx", 1)
    cols, raw, code_rows = call(
        late_tables_kernel,
        [
            shape(2, 8, mig),
            shape(8, wide_total),
            shape(peers, slots, BLK, dtype=I32),
        ],
        state,
        ints,
        tables,
        sent1,
        scratch=[SMEM((peers, BLK), I32), DMA((1,))],
    )
    packs = call(
        export_kernel,
        [
            shape(8, 2 * mig + slots * BLK if q == 0 else packed_width(mig, slots) * BLK)
            for q in range(peers)
        ],
        cols,
        marks1,
        got0,
        got1,
        raw,
        code_rows,
    )
    sent = exchanged(packs, BLOCK_ORDER)
    packed = shape(3 + 2 * 7 + peers, active_ids.shape[2], dtype=I32)
    own, before, near_pick, far_pick, packed = call(
        own_kernel,
        [
            shape(TOTACT, inner, 8, BLK),
            shape(blocks, BLK),
            shape(TOTACT * 8, blocks),
            shape(TOTACT * 8, max(BLK, peers * slots)),
            packed,
        ],
        state,
        got0,
        got1,
        tables,
        active_ids,
        active_count,
        jnp.transpose(local_nbrs, (0, 3, 1, 2)),
        jnp.transpose(ghost_slots, (0, 1, 3, 2)),
        export_blocks,
        scratch=fetch_scratch([packed]),
    )
    local = shape(TOTACT, inner * BLK, BLK)
    remote = shape(TOTACT, 3, (8 - inner) * BLK, BLK)
    near, density, centre, press, inside, outside, *returns = call(
        make_density_kernel(peers, slots),
        [
            shape(TOTACT, 8, 8, BLK),
            shape(blocks, BLK),
            shape(TOTACT, 5, BLK, BLK),
            shape(TOTACT, BLK, BLK),
            local,
            remote,
        ]
        + [shape(8, slots * BLK)] * peers,
        own,
        before,
        tables,
        packed,
        *sent,
        scratch=[
            VMEM((peers, 8, mig), F32),
            VMEM((8, wide_total), F32),
            VMEM((6, BLK, BLK), F32),
            VMEM((6, BLK, BLK), F32),
            VMEM((TOTACT, BLK), F32),
            VMEM((TOTACT, 6 * (8 - inner) * 8, BLK), F32),
            VMEM((TOTACT, 8, 8, BLK), F32),
            VMEM((8, wide_total), F32),
        ]
        + fetch_scratch([packed]),
    )
    got = exchanged(returns, RETURN_ORDER)
    totals, sums = call(
        inner_kernel,
        [shape(8, per_dev), shape(TOTACT, 3, BLK, BLK)],
        near,
        density,
        centre,
        press,
        inside,
        near_pick,
        packed,
        scratch=[
            VMEM((TOTACT, 8, BLK), F32),
            VMEM((TOTACT, 3 * inner * 8, BLK), F32),
            VMEM((TOTACT, 8, 8, BLK), F32),
        ]
        + fetch_scratch([packed]),
    )
    accel, density_out = call(
        make_outer_kernel(peers, slots),
        [shape(3, per_dev), shape(blocks, BLK)],
        near,
        density,
        press,
        outside,
        totals,
        sums,
        far_pick,
        packed,
        *returns,
        *got,
        out_any=True,
        scratch=[
            VMEM((3, per_dev), F32),
            VMEM((max(BLK, peers * slots), BLK), F32),
            VMEM((TOTACT, 8, BLK), F32),
            VMEM((TOTACT, 8, BLK), F32),
            DMA((PIECES + 1,)),
        ]
        + fetch_scratch([packed]),
    )
    return density_out.reshape(-1), accel


def solution(mesh):
    both = ("gx", "gy")
    placed = (
        P(None, both),
        P(both, None),
        P(both, None, None),
        P(both, None, None),
        P(both, None),
        P(both, None, None, None),
        P(both, None, None, None),
        P(both, None, None),
    )
    return jax.shard_map(
        shards,
        mesh=mesh,
        in_specs=placed,
        out_specs=(P(both), P(None, both)),
        check_vma=False,
    )
```
